512 devices in a mesh: section: 4 (over x), seq: 128 (over z, y, core).
Axes of the slice: x: 4, y: 8, z: 8, core: 2. Of those that a mesh axis runs over, the one named last changes fastest.
Arguments:
- hidden: bfloat16 [65536, 4096], P('seq', 'section'), may hold values from -6 to 6
- norm_gain: bfloat16 [4096], P('section'), may hold values from 0.25 to 1.75
- query_weight: bfloat16 [4096, 512], P(None, 'section')
- key_weight: bfloat16 [4096, 128], P('section')
- value_weight: bfloat16 [4096, 128], P('section'), may hold values from -0.5 to 0.5
- output_weight: bfloat16 [512, 4096], P(None, 'section'), may hold values from -0.25 to 0.25
- block_reach: int32 [512], P('seq'), may hold values from 0 to 2
- header_ids: int32 [2], replicated, may hold values from 0 to 511, as said below
Outputs:
- attention_out: bfloat16 [65536, 4096], P('seq', 'section')
The draws below stay inside these ranges and needn't reach their ends.
Inputs may be any that keep to these rules, and one draw needn't show every extreme that they name: `header_ids`: the 2 indices are distinct block indices, and the last block, 511, is always one of them, at any position.
All inputs are finite; a program needn't handle non-finite values.
Results may differ from the reference program's by a relative error of at most 0.014.
Values may be sent and summed in bfloat16 or wider, within the bound.
No kernel may reach another device: no remote copies, remote signals or barrier semaphores. Data moves between devices by JAX's collectives and lax.ppermute only.
A program may use at most 64 MiB of HBM per device.

```python
import math
import jax
import jax.numpy as jnp
from jax import lax

D = 4096
HEAD_DIM = 128
GROUP = 4
BLOCK = 128
REACH = 2
HEADER_BLOCKS = 2
BLOCKS_DEV = 4
ROWS = 512
NBLOCKS = 512
SEQ = 65536
N_SEQ = 128


def draw_query_weight(key, part):
    jitter = jax.random.normal(jax.random.fold_in(key, 12), (D, GROUP * HEAD_DIM), jnp.float32) * (1.0 / math.sqrt(D))
    return jitter.astype(jnp.bfloat16)


def draw_key_weight(key, part):
    jitter = jax.random.normal(jax.random.fold_in(key, 13), (D, HEAD_DIM), jnp.float32) * (2.0 / math.sqrt(D))
    return jitter.astype(jnp.bfloat16)


def draw_header_ids(key, part):
    others = jax.random.permutation(jax.random.fold_in(key, 17), NBLOCKS - 1)[:HEADER_BLOCKS - 1].astype(jnp.int32)
    chosen = jnp.concatenate([others, jnp.full((1,), NBLOCKS - 1, jnp.int32)])
    order = jax.random.permutation(jax.random.fold_in(key, 19), HEADER_BLOCKS).astype(jnp.int32)
    return jnp.take(chosen, order).astype(jnp.int32)


def set_ends(entries, key, low, high):
    longest = entries.shape.index(max(entries.shape))
    spots = []
    for shift in (0, 1):
        where = [jax.random.randint(jax.random.fold_in(key, axis), (), 0, length) for axis, length in enumerate(entries.shape)]
        where[longest] = (where[longest] + shift) % entries.shape[longest]
        spots.append(tuple(where))
    return entries.at[spots[0]].set(low).at[spots[1]].set(high)


def block_levels(rng, shape, cuts, low, high):
    gain = 1.0
    for axis_at, shards_of in cuts:
        steps = jax.random.uniform(jax.random.fold_in(jax.random.fold_in(rng, 6), axis_at), (shards_of,), jnp.float32, low / len(cuts), high / len(cuts))
        gain = gain * jnp.repeat(jnp.exp(steps), shape[axis_at] // shards_of).reshape((-1,) + (1,) * (len(shape) - 1 - axis_at))
    return gain


def centred(key, shape, spread, limit, cuts=(), held_as=jnp.bfloat16):
    values = spread * jax.random.normal(key, shape, jnp.float32)
    if cuts:
        values = values * block_levels(key, shape, cuts, -0.22, 0.18)
    return jnp.clip(values, -limit, limit).astype(held_as)


def setup_inputs(seed: int = 0) -> dict:
    key_list = jax.random.split(jax.random.key(seed), 9)
    return {
        "hidden": centred(key_list[0], (SEQ, D), 1.0, 6.0, ((0, 128), (1, 4))),
        "norm_gain": jnp.clip(1.0 + 0.15 * jax.random.normal(key_list[1], (D,), jnp.float32), 0.25, 1.75).astype(jnp.bfloat16),
        "query_weight": draw_query_weight(jax.random.fold_in(key_list[8], 71), 0),
        "key_weight": draw_key_weight(jax.random.fold_in(key_list[8], 71), 0),
        "value_weight": centred(key_list[4], (D, HEAD_DIM), (D // 32) ** -0.5, 0.5, ((0, 4),)),
        "output_weight": centred(key_list[5], (GROUP * HEAD_DIM, D), (GROUP * HEAD_DIM) ** -0.5, 0.25, ((1, 4),)),
        "block_reach": set_ends(jax.random.randint(key_list[6], (NBLOCKS,), 0, REACH + 1), jax.random.fold_in(key_list[6], 1), 0, REACH).astype(jnp.int32),
        "header_ids": draw_header_ids(jax.random.fold_in(key_list[8], 71), 0),
    }


EPSILON = 1e-05
THETA = 500000.0

def tables(positions, head_width):
    middle = head_width // 2
    frequency = jnp.exp(-(2.0 / head_width) * math.log(THETA) * jnp.arange(middle, dtype=jnp.float32))
    angles = positions.astype(jnp.float32)[:, None] * frequency[None, :]
    angles = jnp.concatenate([angles, angles], axis=1)
    return (jnp.cos(angles), jnp.sin(angles))

def rotate(values, cosine_table, sine_table):
    middle = values.shape[-1] // 2
    turned = jnp.concatenate([-values[..., middle:], values[..., :middle]], axis=-1)
    return values * cosine_table + turned * sine_table

def reference(hidden, norm_gain, query_weight, key_weight, value_weight, output_weight, block_reach, header_ids):
    floats = hidden.astype(jnp.float32)
    scaling = lax.rsqrt(lax.optimization_barrier(jnp.mean(floats * floats, axis=1, keepdims=True)) + EPSILON)
    normed = (floats * scaling * norm_gain.astype(jnp.float32)[None, :]).astype(jnp.bfloat16)
    positions = jnp.arange(SEQ, dtype=jnp.int32)
    cosine_table, sine_table = tables(positions, HEAD_DIM)
    queries = jnp.dot(normed, query_weight, preferred_element_type=jnp.float32).reshape(SEQ, GROUP, HEAD_DIM)
    queries = rotate(queries, cosine_table[:, None, :], sine_table[:, None, :]).astype(jnp.bfloat16)
    keys_all = rotate(jnp.dot(normed, key_weight, preferred_element_type=jnp.float32), cosine_table, sine_table).astype(jnp.bfloat16)
    values_all = jnp.dot(normed, value_weight, preferred_element_type=jnp.float32).astype(jnp.bfloat16)
    header_rows = (header_ids[:, None] * BLOCK + jnp.arange(BLOCK, dtype=jnp.int32)[None, :]).reshape(-1)
    head_queries = queries[header_rows].astype(jnp.float32)
    head_keys = keys_all[header_rows].astype(jnp.float32)
    head_values = values_all[header_rows].astype(jnp.float32)
    inverse_root = 1.0 / math.sqrt(HEAD_DIM)

    def shard_partial(shard_number):
        first_row = (shard_number * ROWS).astype(jnp.int32)
        shard_keys = lax.dynamic_slice_in_dim(keys_all, first_row, ROWS, 0).astype(jnp.float32)
        shard_values = lax.dynamic_slice_in_dim(values_all, first_row, ROWS, 0).astype(jnp.float32)
        scores = jnp.einsum('qgd,kd->gqk', head_queries, shard_keys) * inverse_root
        largest = lax.optimization_barrier(jnp.max(scores, axis=2))
        weights = jnp.exp(scores - largest[:, :, None])
        totals = lax.optimization_barrier(jnp.sum(weights, axis=2))
        rounded = lax.optimization_barrier(weights.astype(jnp.bfloat16)).astype(jnp.float32)
        partial_out = jnp.einsum('gqk,kd->gqd', rounded, shard_values)
        return (largest, totals, partial_out)
    largest, totals, partial_out = lax.map(shard_partial, jnp.arange(N_SEQ, dtype=jnp.int32))
    overall = lax.optimization_barrier(jnp.max(largest, axis=0))
    factors = jnp.exp(largest - overall[None])
    header_out = lax.optimization_barrier(jnp.sum(partial_out * factors[..., None], axis=0)) / lax.optimization_barrier(jnp.sum(totals * factors, axis=0))[..., None]
    margin_rows = REACH * BLOCK
    padded_keys = jnp.pad(keys_all, ((margin_rows, margin_rows), (0, 0)))
    padded_values = jnp.pad(values_all, ((margin_rows, margin_rows), (0, 0)))
    extent = ROWS + 2 * margin_rows

    def shard_window(shard_number):
        first_row = (shard_number * ROWS).astype(jnp.int32)
        near_keys = lax.dynamic_slice_in_dim(padded_keys, first_row, extent, 0).astype(jnp.float32)
        near_values = lax.dynamic_slice_in_dim(padded_values, first_row, extent, 0).astype(jnp.float32)
        key_blocks = shard_number * BLOCKS_DEV - REACH + jnp.arange(extent, dtype=jnp.int32) // BLOCK
        query_blocks = shard_number * BLOCKS_DEV + jnp.arange(ROWS, dtype=jnp.int32) // BLOCK
        limits = block_reach[query_blocks]
        key_header = jnp.any(header_ids[:, None] == key_blocks[None, :], axis=0)
        allowed = (key_blocks >= 0)[None, :] & (key_blocks < NBLOCKS)[None, :]
        allowed = allowed & (jnp.abs(key_blocks[None, :] - query_blocks[:, None]) <= limits[:, None])
        allowed = allowed & jnp.logical_not(key_header)[None, :]
        shard_queries = lax.dynamic_slice_in_dim(queries, first_row, ROWS, 0).astype(jnp.float32)
        near_scores = jnp.einsum('qgd,kd->gqk', shard_queries, near_keys) * inverse_root
        near_scores = jnp.where(allowed[None], near_scores, -jnp.inf)
        far_scores = jnp.einsum('qgd,kd->gqk', shard_queries, head_keys) * inverse_root
        scores = jnp.concatenate([near_scores, far_scores], axis=2)
        row_top = lax.optimization_barrier(jnp.max(scores, axis=2))
        weights = jnp.exp(scores - row_top[..., None])
        row_sums = lax.optimization_barrier(jnp.sum(weights, axis=2))
        rounded = lax.optimization_barrier(weights.astype(jnp.bfloat16)).astype(jnp.float32)
        joined = jnp.concatenate([near_values, head_values], axis=0)
        return jnp.einsum('gqk,kd->qgd', rounded, joined) / jnp.transpose(row_sums)[:, :, None]
    window = lax.map(shard_window, jnp.arange(N_SEQ, dtype=jnp.int32))
    window = window.reshape(NBLOCKS, BLOCK, GROUP, HEAD_DIM)
    header_blocks = jnp.transpose(header_out, (1, 0, 2)).reshape(HEADER_BLOCKS, BLOCK, GROUP, HEAD_DIM)
    window = window.at[header_ids].set(header_blocks)
    attended = window.reshape(SEQ, GROUP * HEAD_DIM).astype(jnp.bfloat16)
    return jnp.dot(attended, output_weight, preferred_element_type=jnp.float32).astype(jnp.bfloat16)
```

```python
import math

import jax
import jax.numpy as jnp
from jax import lax
from jax.sharding import PartitionSpec as P

BLOCK = 128
REACH = 2

EPSILON = 1e-05
THETA = 500000.0


def padded(cells, axis, width):
    count = lax.axis_size(axis)
    ends = count - 1
    head = cells[:width]
    tail = cells[cells.shape[0] - width :]
    return jnp.concatenate(
        [
            lax.ppermute(tail, axis, [(i, i + 1) for i in range(ends)]),
            cells,
            lax.ppermute(head, axis, [(i + 1, i) for i in range(ends)]),
        ],
        axis=0,
    )


def tables(positions, head_width):
    middle = head_width // 2
    frequency = jnp.exp(
        -(2.0 / head_width) * math.log(THETA) * jnp.arange(middle, dtype=jnp.float32)
    )
    angles = positions.astype(jnp.float32)[:, None] * frequency[None, :]
    cosine, sine = jnp.cos(angles), jnp.sin(angles)
    return jnp.concatenate([cosine, cosine], axis=1), jnp.concatenate([-sine, sine], axis=1)


def rotate(values, cosine, signed_sine):
    middle = values.shape[-1] // 2
    turned = jnp.concatenate([values[..., middle:], values[..., :middle]], axis=-1)
    return values * cosine + turned * signed_sine


def split_float(value):
    high = value.astype(jnp.bfloat16)
    low = (value - high.astype(jnp.float32)).astype(jnp.bfloat16)
    return high, low


def to_all(chunk, axis):
    copies = jnp.broadcast_to(chunk[None], (lax.axis_size(axis),) + chunk.shape)
    return lax.all_to_all(copies, axis, 0, 0)


def on_device(
    hidden,
    norm_gain,
    query_weight,
    key_weight,
    value_weight,
    output_weight,
    block_reach,
    header_ids,
):
    bf16, f32 = jnp.bfloat16, jnp.float32
    rows, part = hidden.shape
    head_width = key_weight.shape[1]
    sections = lax.axis_size("section")
    shards = lax.axis_size("seq")
    local_blocks = rows // BLOCK
    total_blocks = local_blocks * shards
    seq_place = lax.axis_index("seq")
    headers = header_ids.shape[0]
    lines = headers * BLOCK // shards // headers
    owners = header_ids // local_blocks
    slots = header_ids % local_blocks

    candidates = jnp.stack(
        [
            lax.dynamic_slice_in_dim(hidden, slots[h] * BLOCK, BLOCK, axis=0)
            for h in range(headers)
        ]
    )
    spread = lax.all_to_all(
        candidates.reshape(headers, shards, lines, part).transpose(1, 0, 2, 3), "seq", 0, 0
    )
    header_rows = jnp.concatenate(
        [
            lax.dynamic_slice_in_dim(spread[:, h], owners[h], 1, axis=0)[0]
            for h in range(headers)
        ]
    )
    head_weights = lax.all_to_all(
        query_weight.reshape(sections, part, head_width), "section", 0, 0
    )

    mine = headers * lines
    everything = jnp.concatenate([hidden, header_rows], axis=0)
    floats = everything.astype(f32)
    gained = (floats * norm_gain.astype(f32)[None, :]).astype(bf16)
    squares = jnp.sum(floats * floats, axis=1)
    high, low = split_float(squares)
    extra = jnp.concatenate(
        [
            jnp.pad(high, (0, -high.shape[0] % head_width)).reshape(-1, head_width),
            jnp.pad(low, (0, -low.shape[0] % head_width)).reshape(-1, head_width),
        ]
    )
    extra = jnp.pad(extra, ((0, 0), (0, 2 * head_width)))
    keyval_weight = jnp.concatenate([key_weight, value_weight], axis=1)
    keyval = jnp.dot(gained, keyval_weight, preferred_element_type=f32).astype(bf16)
    queries_part = jnp.einsum(
        "rd,hde->hre", gained, head_weights, preferred_element_type=f32
    ).astype(bf16)
    payload = jnp.concatenate(
        [
            queries_part,
            jnp.broadcast_to(keyval[None], (sections,) + keyval.shape),
        ],
        axis=2,
    )
    payload = jnp.concatenate(
        [payload, jnp.broadcast_to(extra[None], (sections,) + extra.shape)], axis=1
    )
    arrived = lax.all_to_all(payload, "section", 0, 0)
    total = jnp.sum(arrived.astype(f32), axis=0)
    count = rows + mine
    sums = total[count:, :head_width]
    half = sums.shape[0] // 2
    squares_all = (sums[:half] + sums[half:]).reshape(-1)[:count]
    scaling = lax.rsqrt(squares_all / (part * sections) + EPSILON)
    total = total[:count] * scaling[:, None]

    own_positions = seq_place * rows + jnp.arange(rows, dtype=jnp.int32)
    header_positions = (
        header_ids[:, None] * BLOCK + seq_place * lines + jnp.arange(lines, dtype=jnp.int32)[None]
    ).reshape(-1)
    cosine, sine = tables(jnp.concatenate([own_positions, header_positions]), head_width)
    queries = rotate(total[:, :head_width], cosine, sine).astype(bf16)
    keys = rotate(total[:, head_width : 2 * head_width], cosine, sine).astype(bf16)
    values = total[:, 2 * head_width :].astype(bf16)
    header_chunk = jnp.concatenate([queries[rows:], keys[rows:], values[rows:]], axis=1)
    header_pack = to_all(header_chunk, "seq").reshape(-1, 3 * head_width)
    queries, keys, values = queries[:rows], keys[:rows], values[:rows]
    head_queries = header_pack[:, :head_width]
    head_keys = header_pack[:, head_width : 2 * head_width]
    head_values = header_pack[:, 2 * head_width :]

    inverse_root = 1.0 / math.sqrt(head_width)
    far_scores = (
        jnp.einsum("qd,kd->qk", head_queries, keys, preferred_element_type=f32) * inverse_root
    )
    far_max = jnp.max(far_scores, axis=1, keepdims=True)
    far_weights = jnp.exp(far_scores - far_max)
    far_total = jnp.sum(far_weights, axis=1, keepdims=True)
    far_out = jnp.dot(far_weights.astype(bf16), values, preferred_element_type=f32)
    half_lanes = (far_out.shape[0], head_width // 2)
    partial = jnp.concatenate(
        [
            far_out,
            jnp.broadcast_to(far_max, half_lanes),
            jnp.broadcast_to(far_total, half_lanes),
        ],
        axis=1,
    )
    parts = lax.all_to_all(partial.reshape(shards, mine, 2 * head_width), "seq", 0, 0)
    part_max = parts[..., head_width : head_width + 1]
    part_total = parts[..., head_width + head_width // 2 : head_width + head_width // 2 + 1]
    factor = jnp.exp(part_max - jnp.max(part_max, axis=0, keepdims=True))
    header_result = jnp.sum(parts[..., :head_width] * factor, axis=0) / jnp.sum(
        part_total * factor, axis=0
    )
    header_all = to_all(header_result.astype(bf16), "seq").reshape(
        shards, headers, lines, head_width
    )

    margin_rows = REACH * BLOCK
    extended = padded(jnp.concatenate([keys, values], axis=1), "seq", margin_rows)
    near_keys = extended[:, :head_width]
    near_values = extended[:, head_width:]
    extent = rows + 2 * margin_rows
    key_blocks = seq_place * local_blocks - REACH + jnp.arange(extent, dtype=jnp.int32) // BLOCK
    query_blocks = seq_place * local_blocks + jnp.arange(rows, dtype=jnp.int32) // BLOCK
    limits = jnp.repeat(block_reach, BLOCK)
    key_header = jnp.any(header_ids[:, None] == key_blocks[None, :], axis=0)
    allowed = (key_blocks >= 0)[None, :] & (key_blocks < total_blocks)[None, :]
    allowed = allowed & (jnp.abs(key_blocks[None, :] - query_blocks[:, None]) <= limits[:, None])
    allowed = allowed & jnp.logical_not(key_header)[None, :]
    near_scores = (
        jnp.einsum("qd,kd->qk", queries, near_keys, preferred_element_type=f32) * inverse_root
    )
    near_scores = jnp.where(allowed, near_scores, -jnp.inf)
    head_scores = (
        jnp.einsum("qd,kd->qk", queries, head_keys, preferred_element_type=f32) * inverse_root
    )
    scores = jnp.concatenate([near_scores, head_scores], axis=1)
    row_top = jnp.max(scores, axis=1)
    weights = jnp.exp(scores - row_top[:, None])
    row_sums = jnp.sum(weights, axis=1)
    joined = jnp.concatenate([near_values, head_values], axis=0)
    mixed = (
        jnp.dot(weights.astype(bf16), joined, preferred_element_type=f32) / row_sums[:, None]
    ).astype(bf16)

    blocks = []
    for b in range(local_blocks):
        block = mixed[b * BLOCK : (b + 1) * BLOCK]
        for h in range(headers):
            here = header_ids[h] == seq_place * local_blocks + b
            block = jnp.where(here, header_all[:, h].reshape(BLOCK, head_width), block)
        blocks.append(block)
    attended = jnp.concatenate(blocks, axis=0)
    gathered = lax.all_gather(attended, "section", axis=1, tiled=True)
    return jnp.dot(gathered, output_weight, preferred_element_type=f32).astype(bf16)


def solution(mesh):
    return jax.shard_map(
        on_device,
        mesh=mesh,
        in_specs=(
            P("seq", "section"),
            P("section"),
            P(None, "section"),
            P("section", None),
            P("section", None),
            P(None, "section"),
            P("seq"),
            P(),
        ),
        out_specs=P("seq", "section"),
        check_vma=False,
    )
```

```python
import math

import jax
import jax.numpy as jnp
from jax import lax
from jax.sharding import PartitionSpec as P

BLOCK = 128
REACH = 2

EPSILON = 1e-05
THETA = 500000.0


def shift(value, axis, by):
    count = lax.axis_size(axis)
    return lax.ppermute(value, axis, [(i, (i + by) % count) for i in range(count)])


def tables(positions, head_width):
    middle = head_width // 2
    frequency = jnp.exp(
        -(2.0 / head_width) * math.log(THETA) * jnp.arange(middle, dtype=jnp.float32)
    )
    angles = positions.astype(jnp.float32)[:, None] * frequency[None, :]
    cosine, sine = jnp.cos(angles), jnp.sin(angles)
    return jnp.concatenate([cosine, cosine], axis=1), jnp.concatenate([-sine, sine], axis=1)


def rotate(values, cosine, signed_sine):
    middle = values.shape[-1] // 2
    turned = jnp.concatenate([values[..., middle:], values[..., :middle]], axis=-1)
    return values * cosine + turned * signed_sine


def project(total, cosine, sine, head_width):
    bf16 = jnp.bfloat16
    queries = rotate(total[:, :head_width], cosine, sine).astype(bf16)
    keys = rotate(total[:, head_width : 2 * head_width], cosine, sine).astype(bf16)
    return queries, keys, total[:, 2 * head_width :].astype(bf16)


def on_device(
    hidden,
    norm_gain,
    query_weight,
    key_weight,
    value_weight,
    output_weight,
    block_reach,
    header_ids,
):
    bf16, f32 = jnp.bfloat16, jnp.float32
    rows, part = hidden.shape
    head_width = key_weight.shape[1]
    sections = lax.axis_size("section")
    shards = lax.axis_size("seq")
    local_blocks = rows // BLOCK
    total_blocks = local_blocks * shards
    section_place = lax.axis_index("section")
    seq_place = lax.axis_index("seq")
    headers = header_ids.shape[0]
    lines = BLOCK // shards
    mine = headers * lines
    owners = header_ids // local_blocks
    slots = header_ids % local_blocks
    width = part * sections
    gain = norm_gain.astype(f32)[None, :]

    candidates = jnp.concatenate(
        [
            lax.dynamic_slice_in_dim(hidden, slots[h] * BLOCK, BLOCK, axis=0).reshape(
                shards, lines, part
            )
            for h in range(headers)
        ],
        axis=1,
    )
    spread = lax.all_to_all(candidates, "seq", 0, 0)

    head_weights = []
    for k in range(sections):
        target = (section_place + k) % sections
        piece = lax.dynamic_slice_in_dim(query_weight, target * part, part, axis=0)
        head_weights.append(shift(piece, "section", k) if k else piece)

    floats = hidden.astype(f32)
    squares = lax.psum(jnp.sum(floats * floats, axis=1), "section")
    scaling = lax.rsqrt(squares / width + EPSILON)
    normed = (floats * scaling[:, None] * gain).astype(bf16)
    keyval_weight = jnp.concatenate([key_weight, value_weight], axis=1)

    header_rows = jnp.concatenate(
        [
            lax.dynamic_slice_in_dim(spread, owners[h], 1, axis=0)[
                0, h * lines : (h + 1) * lines
            ]
            for h in range(headers)
        ]
    ).astype(f32)
    gained = header_rows * gain
    gained_high = gained.astype(bf16)
    gained_low = (gained - gained_high.astype(f32)).astype(bf16)
    gained = jnp.concatenate([gained_high, gained_low])
    both = [
        jnp.dot(gained, weight, preferred_element_type=f32)
        for weight in head_weights + [keyval_weight]
    ]
    both = [value[:mine] + value[mine:] for value in both]
    header_squares = jnp.broadcast_to(
        jnp.sum(header_rows * header_rows, axis=1, keepdims=True), (mine, head_width)
    )
    chunks = []
    for target in range(sections):
        which = (section_place - target) % sections
        query_part = sum(jnp.where(which == k, both[k], 0.0) for k in range(sections))
        chunks.append(jnp.concatenate([query_part, both[sections], header_squares], axis=1))
    header_arrived = jnp.sum(lax.all_to_all(jnp.stack(chunks), "section", 0, 0), axis=0)
    header_scaling = lax.rsqrt(header_arrived[:, 3 * head_width :] / width + EPSILON)
    header_total = header_arrived[:, : 3 * head_width] * jnp.concatenate(
        [header_scaling] * 3, axis=1
    )
    header_positions = (
        header_ids[:, None] * BLOCK + seq_place * lines + jnp.arange(lines, dtype=jnp.int32)[None]
    ).reshape(-1)
    header_tables = tables(header_positions, head_width)
    header_chunk = jnp.concatenate(
        project(header_total, *header_tables, head_width), axis=1
    )
    keyval = jnp.dot(normed, keyval_weight, preferred_element_type=f32)
    total = jnp.concatenate(
        [jnp.dot(normed, head_weights[0], preferred_element_type=f32), keyval], axis=1
    )
    sends = [
        jnp.concatenate(
            [jnp.dot(normed, head_weights[k], preferred_element_type=f32), keyval], axis=1
        ).astype(bf16)
        for k in range(1, sections)
    ]
    header_chunk, *sends = lax.optimization_barrier((header_chunk, *sends))
    header_pack = lax.all_to_all(
        jnp.broadcast_to(header_chunk[None], (shards,) + header_chunk.shape), "seq", 0, 0
    ).reshape(-1, 3 * head_width)
    arrivals = [shift(sends[k - 1], "section", -k) for k in range(1, sections)]
    header_pack, *arrivals = lax.optimization_barrier((header_pack, *arrivals))
    for arrival in arrivals:
        total = total + arrival.astype(f32)
    own_positions = seq_place * rows + jnp.arange(rows, dtype=jnp.int32)
    queries, keys, values = project(total, *tables(own_positions, head_width), head_width)

    head_queries = header_pack[:, :head_width]
    head_keys = header_pack[:, head_width : 2 * head_width]
    head_values = header_pack[:, 2 * head_width :]

    inverse_root = 1.0 / math.sqrt(head_width)
    far_scores = (
        jnp.einsum("qd,kd->qk", head_queries, keys, preferred_element_type=f32) * inverse_root
    )
    far_max = jnp.max(far_scores, axis=1, keepdims=True)
    far_weights = jnp.exp(far_scores - far_max)
    far_total = jnp.sum(far_weights, axis=1, keepdims=True)
    far_out = jnp.dot(far_weights.astype(bf16), values, preferred_element_type=f32) / far_total
    far_level = far_max + jnp.log(far_total)
    first = far_level.astype(bf16).astype(f32)
    second = (far_level - first).astype(bf16).astype(f32)
    third = far_level - first - second
    lane = lax.broadcasted_iota(jnp.int32, far_out.shape, 1)
    level = jnp.where(lane < 32, first, jnp.where(lane < 64, second, third))
    partial = jnp.concatenate(
        [
            far_out.astype(bf16).reshape(shards, mine, head_width),
            level.astype(bf16).reshape(shards, mine, head_width),
        ],
        axis=1,
    )
    stacked = jnp.concatenate([keys, values], axis=1)
    partial, queries, stacked = lax.optimization_barrier((partial, queries, stacked))
    parts = lax.all_to_all(partial, "seq", 0, 0).astype(f32)
    levels = parts[:, mine:, 0:1] + parts[:, mine:, 32:33] + parts[:, mine:, 64:65]
    factor = jnp.exp(levels - jnp.max(levels, axis=0, keepdims=True))
    header_result = jnp.sum(parts[:, :mine] * factor, axis=0) / jnp.sum(factor, axis=0)
    everywhere = sections * shards
    header_all = lax.all_to_all(
        jnp.broadcast_to(
            header_result.astype(bf16)[None], (everywhere, mine, head_width)
        ),
        ("section", "seq"),
        0,
        0,
    ).reshape(sections, shards, headers, lines, head_width)

    margin_rows = REACH * BLOCK
    extended = jnp.concatenate(
        [
            shift(stacked[rows - margin_rows :], "seq", 1),
            stacked,
            shift(stacked[:margin_rows], "seq", -1),
        ]
    )
    near_keys = extended[:, :head_width]
    near_values = extended[:, head_width:]
    extent = rows + 2 * margin_rows
    key_blocks = seq_place * local_blocks - REACH + jnp.arange(extent, dtype=jnp.int32) // BLOCK
    query_blocks = seq_place * local_blocks + jnp.arange(rows, dtype=jnp.int32) // BLOCK
    limits = jnp.repeat(block_reach, BLOCK)
    key_header = jnp.any(header_ids[:, None] == key_blocks[None, :], axis=0)
    allowed = (key_blocks >= 0)[None, :] & (key_blocks < total_blocks)[None, :]
    allowed = allowed & (jnp.abs(key_blocks[None, :] - query_blocks[:, None]) <= limits[:, None])
    allowed = allowed & jnp.logical_not(key_header)[None, :]
    near_scores = (
        jnp.einsum("qd,kd->qk", queries, near_keys, preferred_element_type=f32) * inverse_root
    )
    near_scores = jnp.where(allowed, near_scores, -jnp.inf)
    head_scores = (
        jnp.einsum("qd,kd->qk", queries, head_keys, preferred_element_type=f32) * inverse_root
    )
    scores = jnp.concatenate([near_scores, head_scores], axis=1)
    row_top = jnp.max(scores, axis=1)
    weights = jnp.exp(scores - row_top[:, None])
    row_sums = jnp.sum(weights, axis=1)
    joined = jnp.concatenate([near_values, head_values], axis=0)
    mixed = (
        jnp.dot(weights.astype(bf16), joined, preferred_element_type=f32) / row_sums[:, None]
    ).astype(bf16)
    result = None
    for k in range(sections):
        piece = shift(mixed, "section", k) if k else mixed
        source = (section_place - k) % sections
        matrix = lax.dynamic_slice_in_dim(output_weight, source * head_width, head_width, axis=0)
        product = jnp.dot(piece, matrix, preferred_element_type=f32)
        result = product if result is None else result + product
    result = result.astype(bf16)

    for h in range(headers):
        attended = jnp.concatenate(
            [header_all[s, :, h].reshape(BLOCK, head_width) for s in range(sections)], axis=1
        )
        block = jnp.dot(attended, output_weight, preferred_element_type=f32).astype(bf16)
        place = slots[h] * BLOCK
        present = lax.dynamic_slice_in_dim(result, place, BLOCK, axis=0)
        block = jnp.where(owners[h] == seq_place, block, present)
        result = lax.dynamic_update_slice_in_dim(result, block, place, axis=0)
    return result


def solution(mesh):
    return jax.shard_map(
        on_device,
        mesh=mesh,
        in_specs=(
            P("seq", "section"),
            P("section"),
            P(None, "section"),
            P("section", None),
            P("section", None),
            P(None, "section"),
            P("seq"),
            P(),
        ),
        out_specs=P("seq", "section"),
        check_vma=False,
    )
```

```python
import math

import jax
import jax.numpy as jnp
from jax import lax
from jax.sharding import PartitionSpec as P

BLOCK = 128
REACH = 2

EPSILON = 1e-05
THETA = 500000.0


def shift(value, axis, by):
    count = lax.axis_size(axis)
    return lax.ppermute(value, axis, [(i, (i + by) % count) for i in range(count)])


def tables(positions, head_width):
    middle = head_width // 2
    frequency = jnp.exp(
        -(2.0 / head_width) * math.log(THETA) * jnp.arange(middle, dtype=jnp.float32)
    )
    angles = positions.astype(jnp.float32)[:, None] * frequency[None, :]
    cosine, sine = jnp.cos(angles), jnp.sin(angles)
    return jnp.concatenate([cosine, cosine], axis=1), jnp.concatenate([-sine, sine], axis=1)


def rotate(values, cosine, signed_sine):
    middle = values.shape[-1] // 2
    turned = jnp.concatenate([values[..., middle:], values[..., :middle]], axis=-1)
    return values * cosine + turned * signed_sine


def project(total, cosine, sine, head_width):
    bf16 = jnp.bfloat16
    queries = rotate(total[:, :head_width], cosine, sine).astype(bf16)
    keys = rotate(total[:, head_width : 2 * head_width], cosine, sine).astype(bf16)
    return queries, keys, total[:, 2 * head_width :].astype(bf16)


def on_device(
    hidden,
    norm_gain,
    query_weight,
    key_weight,
    value_weight,
    output_weight,
    block_reach,
    header_ids,
):
    bf16, f32 = jnp.bfloat16, jnp.float32
    rows, part = hidden.shape
    head_width = key_weight.shape[1]
    sections = lax.axis_size("section")
    shards = lax.axis_size("seq")
    local_blocks = rows // BLOCK
    total_blocks = local_blocks * shards
    section_place = lax.axis_index("section")
    seq_place = lax.axis_index("seq")
    headers = header_ids.shape[0]
    lines = BLOCK // shards
    mine = headers * lines
    owners = header_ids // local_blocks
    slots = header_ids % local_blocks
    width = part * sections
    gain = norm_gain.astype(f32)[None, :]

    candidates = jnp.concatenate(
        [
            lax.dynamic_slice_in_dim(hidden, slots[h] * BLOCK, BLOCK, axis=0).reshape(
                shards, lines, part
            )
            for h in range(headers)
        ],
        axis=1,
    )
    spread = lax.all_to_all(candidates, "seq", 0, 0)

    floats = hidden.astype(f32)
    squares = jnp.sum(floats * floats, axis=1).reshape(-1, head_width)
    squares_high = squares.astype(bf16)
    squares_low = (squares - squares_high.astype(f32)).astype(bf16)
    square_rows = squares.shape[0]
    head_weights = []
    for k in range(sections):
        target = (section_place + k) % sections
        piece = lax.dynamic_slice_in_dim(query_weight, target * part, part, axis=0)
        if k:
            piece = jnp.concatenate([piece, squares_high, squares_low])
            piece = shift(piece, "section", k)
            tail = piece[part:].astype(f32)
            squares = squares + tail[:square_rows] + tail[square_rows:]
            piece = piece[:part]
        head_weights.append(piece)
    scaling = lax.rsqrt(squares.reshape(-1) / width + EPSILON)
    normed = (floats * scaling[:, None] * gain).astype(bf16)

    header_rows = jnp.concatenate(
        [
            lax.dynamic_slice_in_dim(spread, owners[h], 1, axis=0)[
                0, h * lines : (h + 1) * lines
            ]
            for h in range(headers)
        ]
    ).astype(f32)
    gained = header_rows * gain
    gained_high = gained.astype(bf16)
    gained_low = (gained - gained_high.astype(f32)).astype(bf16)
    left = jnp.concatenate([normed, gained_high, gained_low])
    header_squares = jnp.broadcast_to(
        jnp.sum(header_rows * header_rows, axis=1, keepdims=True), (mine, head_width)
    )
    products = [
        jnp.dot(left, weight, preferred_element_type=f32)
        for weight in head_weights + [key_weight, value_weight]
    ]
    mains = [value[:rows].astype(bf16) for value in products]
    smalls = [value[rows : rows + mine] + value[rows + mine :] for value in products]
    highs = [value.astype(bf16) for value in smalls + [header_squares]]
    lows = [
        (value - high.astype(f32)).astype(bf16)
        for value, high in zip(smalls + [header_squares], highs)
    ]
    used = 3 * rows + 8 * mine
    filler = jnp.zeros((-used % BLOCK, head_width), bf16)
    chunks = []
    for target in range(sections):
        which = (section_place - target) % sections

        def chosen(options):
            value = options[0]
            for k in range(1, sections):
                value = jnp.where(which == k, options[k], value)
            return value

        chunks.append(
            jnp.concatenate(
                [chosen(mains), mains[sections], mains[sections + 1]]
                + [chosen(highs)]
                + highs[sections:]
                + [chosen(lows)]
                + lows[sections:]
                + [filler]
            )
        )
    arrived = lax.all_to_all(jnp.stack(chunks), "section", 0, 0)
    total = jnp.sum(arrived[:, :used].astype(f32), axis=0)
    small = total[3 * rows :]
    small = (small[: 4 * mine] + small[4 * mine :]).reshape(4, mine, head_width)
    small = small[:3] * lax.rsqrt(small[3] / width + EPSILON)
    total = jnp.concatenate([total[k * rows : (k + 1) * rows] for k in range(3)], axis=1)
    header_total = jnp.concatenate([small[0], small[1], small[2]], axis=1)

    header_positions = (
        header_ids[:, None] * BLOCK + seq_place * lines + jnp.arange(lines, dtype=jnp.int32)[None]
    ).reshape(-1)
    header_chunk = jnp.concatenate(
        project(header_total, *tables(header_positions, head_width), head_width), axis=1
    )
    header_pack = lax.all_to_all(
        jnp.broadcast_to(header_chunk[None], (shards,) + header_chunk.shape), "seq", 0, 0
    ).reshape(-1, 3 * head_width)
    own_positions = seq_place * rows + jnp.arange(rows, dtype=jnp.int32)
    queries, keys, values = project(total, *tables(own_positions, head_width), head_width)
    stacked = jnp.concatenate([keys, values], axis=1)
    head_queries = header_pack[:, :head_width]
    head_keys = header_pack[:, head_width : 2 * head_width]
    head_values = header_pack[:, 2 * head_width :]

    inverse_root = 1.0 / math.sqrt(head_width)
    far_scores = (
        jnp.einsum("qd,kd->qk", head_queries, keys, preferred_element_type=f32) * inverse_root
    )
    far_max = jnp.max(far_scores, axis=1, keepdims=True)
    far_weights = jnp.exp(far_scores - far_max)
    far_total = jnp.sum(far_weights, axis=1, keepdims=True)
    far_out = jnp.dot(far_weights.astype(bf16), values, preferred_element_type=f32) / far_total
    far_level = far_max + jnp.log(far_total)
    first = far_level.astype(bf16).astype(f32)
    second = (far_level - first).astype(bf16).astype(f32)
    third = far_level - first - second
    lane = lax.broadcasted_iota(jnp.int32, far_out.shape, 1)
    level = jnp.where(lane < 32, first, jnp.where(lane < 64, second, third))
    partial = jnp.concatenate([far_out, level], axis=1).astype(bf16)
    partial, queries = lax.optimization_barrier((partial, queries))
    parts = lax.all_to_all(partial.reshape(shards, mine, 2 * head_width), "seq", 0, 0)
    parts = parts.astype(f32)
    levels = sum(parts[..., head_width + lane : head_width + lane + 1] for lane in (0, 32, 64))
    factor = jnp.exp(levels - jnp.max(levels, axis=0, keepdims=True))
    header_result = jnp.sum(parts[..., :head_width] * factor, axis=0) / jnp.sum(factor, axis=0)
    header_all = lax.all_to_all(
        jnp.broadcast_to(header_result.astype(bf16)[None], (shards, mine, head_width)),
        "seq",
        0,
        0,
    ).reshape(shards, headers, lines, head_width)

    margin_rows = REACH * BLOCK
    extended = jnp.concatenate(
        [
            shift(stacked[rows - margin_rows :], "seq", 1),
            stacked,
            shift(stacked[:margin_rows], "seq", -1),
        ]
    )
    near_keys = extended[:, :head_width]
    near_values = extended[:, head_width:]
    extent = rows + 2 * margin_rows
    key_blocks = seq_place * local_blocks - REACH + jnp.arange(extent, dtype=jnp.int32) // BLOCK
    query_blocks = seq_place * local_blocks + jnp.arange(rows, dtype=jnp.int32) // BLOCK
    limits = jnp.repeat(block_reach, BLOCK)
    key_header = jnp.any(header_ids[:, None] == key_blocks[None, :], axis=0)
    allowed = (key_blocks >= 0)[None, :] & (key_blocks < total_blocks)[None, :]
    allowed = allowed & (jnp.abs(key_blocks[None, :] - query_blocks[:, None]) <= limits[:, None])
    allowed = allowed & jnp.logical_not(key_header)[None, :]
    near_scores = (
        jnp.einsum("qd,kd->qk", queries, near_keys, preferred_element_type=f32) * inverse_root
    )
    near_scores = jnp.where(allowed, near_scores, -jnp.inf)
    head_scores = (
        jnp.einsum("qd,kd->qk", queries, head_keys, preferred_element_type=f32) * inverse_root
    )
    scores = jnp.concatenate([near_scores, head_scores], axis=1)
    row_top = jnp.max(scores, axis=1)
    weights = jnp.exp(scores - row_top[:, None])
    row_sums = jnp.sum(weights, axis=1)
    joined = jnp.concatenate([near_values, head_values], axis=0)
    mixed = (
        jnp.dot(weights.astype(bf16), joined, preferred_element_type=f32) / row_sums[:, None]
    ).astype(bf16)

    blocks = []
    for b in range(local_blocks):
        block = mixed[b * BLOCK : (b + 1) * BLOCK]
        for h in range(headers):
            here = header_ids[h] == seq_place * local_blocks + b
            block = jnp.where(here, header_all[:, h].reshape(BLOCK, head_width), block)
        blocks.append(block)
    attended = jnp.concatenate(blocks, axis=0)
    gathered = lax.all_gather(attended, "section", axis=1, tiled=True)
    return jnp.dot(gathered, output_weight, preferred_element_type=f32).astype(bf16)


def solution(mesh):
    return jax.shard_map(
        on_device,
        mesh=mesh,
        in_specs=(
            P("seq", "section"),
            P("section"),
            P(None, "section"),
            P("section", None),
            P("section", None),
            P(None, "section"),
            P("seq"),
            P(),
        ),
        out_specs=P("seq", "section"),
        check_vma=False,
    )
```

```python
import functools
import math

import jax
import jax.numpy as jnp
from jax import lax
from jax.experimental import pallas as pl
from jax.experimental.pallas import tpu as pltpu
from jax.sharding import PartitionSpec as P

BLOCK = 128
REACH = 2

EPSILON = 1e-05
THETA = 500000.0


def shift(value, axis, by):
    count = lax.axis_size(axis)
    return lax.ppermute(value, axis, [(i, (i + by) % count) for i in range(count)])


def tables(positions, head_width):
    middle = head_width // 2
    frequency = jnp.exp(
        -(2.0 / head_width) * math.log(THETA) * jnp.arange(middle, dtype=jnp.float32)
    )
    angles = positions.astype(jnp.float32)[:, None] * frequency[None, :]
    cosine, sine = jnp.cos(angles), jnp.sin(angles)
    return jnp.concatenate([cosine, cosine], axis=1), jnp.concatenate([-sine, sine], axis=1)

BF16, F32 = jnp.bfloat16, jnp.float32
VMEM_LIMIT = 48 * 1024 * 1024


def call(kernel, outs, scalars, arrays, scratch=(), blocks=None, aliases=None, anywhere=()):
    whole = pl.BlockSpec(memory_space=pltpu.VMEM)
    specs = [pl.BlockSpec(memory_space=pltpu.SMEM)] * len(scalars)
    specs += [
        pl.BlockSpec(memory_space=pl.ANY) if i in anywhere else whole for i in range(len(arrays))
    ]
    out_specs = [pl.BlockSpec(memory_space=pl.ANY) if aliases else whole for _ in outs]
    return pl.pallas_call(
        kernel,
        out_shape=[jax.ShapeDtypeStruct(shape, dtype) for shape, dtype in outs],
        in_specs=specs,
        out_specs=out_specs,
        scratch_shapes=list(scratch),
        input_output_aliases=aliases or {},
        compiler_params=pltpu.CompilerParams(vmem_limit_bytes=VMEM_LIMIT),
    )(*scalars, *arrays)


def turn(values, cosine, signed_sine):
    return values * cosine + pltpu.roll(values, values.shape[1] // 2, axis=1) * signed_sine


def spread_down(row, size):
    return jnp.transpose(jnp.broadcast_to(row, (size, size)))


def outgoing_kernel(sections, place, x, gain, query_weight, keyval_weight, *refs):
    outs, (keyval_own, squares_own, keyval, rows16) = refs[: sections - 1], refs[sections - 1 :]
    rows, part = x.shape
    size = BLOCK
    count = rows // size
    rows16[...] = jnp.zeros_like(rows16)
    squares_own[...] = jnp.zeros_like(squares_own)
    for b in range(count):
        block = x[b * size : (b + 1) * size, :].astype(F32)
        total = jnp.sum(block * block, axis=1, keepdims=True)
        line = jnp.transpose(jnp.broadcast_to(total, (size, size)))[0:1, :]
        high = line.astype(BF16).astype(F32)
        squares_own[b : b + 1, :] = line
        rows16[b : b + 1, :] = high
        rows16[count + b : count + b + 1, :] = line - high
        block = block * gain[...]
        high = block.astype(BF16)
        low = (block - high.astype(F32)).astype(BF16)
        both = jnp.dot(
            jnp.concatenate([high, low], axis=0), keyval_weight[...], preferred_element_type=F32
        )
        keyval[b * size : (b + 1) * size, :] = both[:size] + both[size:]
    here = place[0]
    keyval_own[...] = keyval[pl.ds(pl.multiple_of(here * size, size), size), :]
    width = keyval.shape[1] // 2
    for k in range(1, sections):
        target = lax.rem(here + k, sections)
        out = outs[k - 1]
        out[0:part, :] = query_weight[pl.ds(pl.multiple_of(target * part, part), part), :]
        block = keyval[pl.ds(pl.multiple_of(target * size, size), size), :].astype(BF16)
        out[part : part + size, :] = block[:, :width]
        out[part + size : part + 2 * size, :] = block[:, width:]
        out[part + 2 * size : part + 2 * size + 16, :] = rows16[...].astype(BF16)


def partial_kernel(
    sections, place, x, gain, query_weight, keyval_own, squares_own, cosine, sine, *refs
):
    arrived, (out, squares, normed) = refs[: sections - 1], refs[sections - 1 :]
    rows, part = x.shape
    size = BLOCK
    count = rows // size
    here = place[0]
    total = squares_own[0:count, :]
    keyval = keyval_own[...]
    for piece in arrived:
        tail = piece[part + 2 * size : part + 2 * size + 16, :].astype(F32)
        total = total + tail[0:count, :] + tail[count : 2 * count, :]
        keyval = keyval + jnp.concatenate(
            [
                piece[part : part + size, :].astype(F32),
                piece[part + size : part + 2 * size, :].astype(F32),
            ],
            axis=1,
        )
    squares[0:count, :] = lax.rsqrt(total / (part * sections) + EPSILON)
    for b in range(count):
        scale = spread_down(squares[b : b + 1, :], size)
        scale = jnp.concatenate([scale] * (part // size), axis=1)
        block = x[b * size : (b + 1) * size, :].astype(F32) * scale * gain[...]
        normed[b * size : (b + 1) * size, :] = block.astype(BF16)
    weights = [query_weight[pl.ds(pl.multiple_of(here * part, part), part), :]]
    weights += [piece[0:part, :] for piece in arrived]
    head_width = query_weight.shape[1]
    for k in range(0, sections, 2):
        pair = jnp.concatenate(weights[k : k + 2], axis=1)
        value = jnp.dot(normed[...], pair, preferred_element_type=F32).astype(BF16)
        for j in range(2):
            target = lax.rem(here - k - j + sections, sections)
            out[target, 0:rows, :] = value[:, j * head_width : (j + 1) * head_width]
    scale = spread_down(squares[pl.ds(here, 1), :], size)
    keys = turn(keyval[:, :head_width] * scale, cosine[...], sine[...]).astype(BF16)
    values = (keyval[:, head_width:] * scale).astype(BF16)
    for target in range(sections):
        out[target, rows : rows + size, :] = keys
        out[target, rows + size : rows + 2 * size, :] = values
        out[target, rows + 2 * size : rows + 2 * size + 16, :] = jnp.zeros(
            (16, head_width), BF16
        )


def header_kernel(
    sections, offset, place, owners, spread, gain, query_weight, keyval_weight, *refs
):
    arrived, (_, out, small, semaphore) = refs[: sections - 1], refs[sections - 1 :]
    part = gain.shape[1]
    head_width = query_weight.shape[1]
    here = place[0]
    row = lax.broadcasted_iota(jnp.int32, (16, part), 0)
    pair = [spread[owners[h]].astype(F32) for h in range(2)]
    line = jnp.where(lax.rem(row, 2) == 0, pair[0][0:1, :], pair[1][1:2, :])
    gained = line * gain[...]
    high = gained.astype(BF16)
    low = (gained - high.astype(F32)).astype(BF16)
    left = jnp.concatenate([high, low], axis=0)
    squares = jnp.broadcast_to(jnp.sum(line * line, axis=1, keepdims=True), (16, head_width))
    row = lax.broadcasted_iota(jnp.int32, (16, head_width), 0)

    def product(weight):
        both = jnp.dot(left, weight, preferred_element_type=F32)
        return both[:16] + both[16:]

    keyval = product(keyval_weight[...])
    weights = [query_weight[pl.ds(pl.multiple_of(here * part, part), part), :]]
    weights += [piece[0:part, :] for piece in arrived]
    for k in range(0, sections, 2):
        queries = product(jnp.concatenate(weights[k : k + 2], axis=1))
        for j in range(2):
            target = lax.rem(here - k - j + sections, sections)
            value = jnp.where(
                row < 4,
                queries[:, j * head_width : (j + 1) * head_width],
                jnp.where(
                    row < 8,
                    keyval[:, :head_width],
                    jnp.where(row < 12, keyval[:, head_width:], squares),
                ),
            )
            high = value.astype(BF16).astype(F32)
            value = jnp.where(lax.rem(row, 4) < 2, high, value - high)
            small[target] = value.astype(BF16)
    copy = pltpu.make_async_copy(small, out.at[:, pl.ds(offset, 16), :], semaphore)
    copy.start()
    copy.wait()


def header_finish_kernel(width, arrived, cosine, sine, out):
    total = jnp.sum(arrived[...].astype(F32), axis=0)
    total = total + pltpu.roll(total, 14, axis=0)
    scale = lax.rsqrt(pltpu.roll(total, 4, axis=0) / width + EPSILON)
    queries = turn(total * scale, cosine[...], sine[...])
    keys = turn(pltpu.roll(total, 12, axis=0) * scale, cosine[...], sine[...])
    values = pltpu.roll(total, 8, axis=0) * scale
    chunk = jnp.concatenate([queries, keys, values], axis=1)[0:2, :].astype(BF16)
    out[...] = jnp.broadcast_to(chunk[None], out.shape)


def main_finish_kernel(arrived, cosine, sine, queries, keyval):
    rows, head_width = queries.shape
    size = BLOCK
    for b in range(rows // size):
        part = slice(b * size, (b + 1) * size)
        total = jnp.sum(arrived[:, part, :].astype(F32), axis=0)
        queries[part, :] = turn(total, cosine[part, :], sine[part, :]).astype(BF16)
        keyval[part, 0:head_width] = arrived[b, rows : rows + size, :]
        keyval[part, head_width:] = arrived[b, rows + size : rows + 2 * size, :]


def merge_kernel(parts, out):
    head_width = out.shape[2]
    everything = parts[...].astype(F32)
    level = everything[:, :, head_width:]
    level = level[:, :, 0:1] + level[:, :, 32:33] + level[:, :, 64:65]
    factor = jnp.exp(level - jnp.max(level, axis=0, keepdims=True))
    total = jnp.sum(everything[:, :, :head_width] * factor, axis=0)
    result = (total / jnp.sum(factor, axis=0)).astype(BF16)
    out[...] = jnp.broadcast_to(result[None], out.shape)


def on_device(
    hidden,
    norm_gain,
    query_weight,
    key_weight,
    value_weight,
    output_weight,
    block_reach,
    header_ids,
):
    bf16, f32 = jnp.bfloat16, jnp.float32
    rows, part = hidden.shape
    head_width = key_weight.shape[1]
    sections = lax.axis_size("section")
    shards = lax.axis_size("seq")
    local_blocks = rows // BLOCK
    total_blocks = local_blocks * shards
    section_place = lax.axis_index("section")
    seq_place = lax.axis_index("seq")
    headers = header_ids.shape[0]
    lines = BLOCK // shards
    mine = headers * lines
    owners = header_ids // local_blocks
    slots = header_ids % local_blocks
    width = part * sections
    gain = norm_gain.astype(f32)[None, :]

    candidates = jnp.concatenate(
        [
            lax.dynamic_slice_in_dim(hidden, slots[h] * BLOCK, BLOCK, axis=0).reshape(
                shards, lines, part
            )
            for h in range(headers)
        ],
        axis=1,
    )
    spread = lax.all_to_all(candidates, "seq", 0, 0)

    place = section_place.astype(jnp.int32).reshape(1)
    keyval_weight = jnp.concatenate([key_weight, value_weight], axis=1)
    tall = part + 2 * BLOCK + 16
    *outgoing, keyval_own, squares_own = call(
        functools.partial(outgoing_kernel, sections),
        [((tall, head_width), bf16)] * (sections - 1)
        + [((BLOCK, 2 * head_width), f32), ((8, head_width), f32)],
        [place],
        [hidden, gain, query_weight, keyval_weight],
        [pltpu.VMEM((rows, 2 * head_width), f32), pltpu.VMEM((16, head_width), f32)],
    )
    incoming = [shift(outgoing[k - 1], "section", k) for k in range(1, sections)]
    own_positions = seq_place * rows + jnp.arange(rows, dtype=jnp.int32)
    own_tables = tables(own_positions, head_width)
    block_tables = [
        lax.dynamic_slice_in_dim(table, section_place * BLOCK, BLOCK, axis=0)
        for table in own_tables
    ]
    length = rows + 2 * BLOCK + 16
    (payload,) = call(
        functools.partial(partial_kernel, sections),
        [((sections, length, head_width), bf16)],
        [place],
        [hidden, gain, query_weight, keyval_own, squares_own, *block_tables, *incoming],
        [pltpu.VMEM((8, head_width), f32), pltpu.VMEM((rows, part), bf16)],
    )
    (payload,) = call(
        functools.partial(header_kernel, sections, length - 16),
        [((sections, length, head_width), bf16)],
        [place, owners],
        [spread, gain, query_weight, keyval_weight, *incoming, payload],
        [pltpu.VMEM((sections, 16, head_width), bf16), pltpu.SemaphoreType.DMA],
        aliases={5 + sections: 0},
        anywhere=(3 + sections,),
    )
    arrived = lax.all_to_all(payload, "section", 0, 0)

    index = jnp.arange(16, dtype=jnp.int32) % 2
    header_positions = jnp.where(index == 0, header_ids[0], header_ids[1]) * BLOCK + seq_place
    (header_copies,) = call(
        functools.partial(header_finish_kernel, width),
        [((shards, mine, 3 * head_width), bf16)],
        [],
        [arrived[:, length - 16 :], *tables(header_positions, head_width)],
    )
    header_pack = lax.all_to_all(header_copies, "seq", 0, 0).reshape(-1, 3 * head_width)
    queries, stacked = call(
        main_finish_kernel,
        [((rows, head_width), bf16), ((rows, 2 * head_width), bf16)],
        [],
        [arrived, *own_tables],
    )
    keys, values = stacked[:, :head_width], stacked[:, head_width:]
    head_queries = header_pack[:, :head_width]
    head_keys = header_pack[:, head_width : 2 * head_width]
    head_values = header_pack[:, 2 * head_width :]

    inverse_root = 1.0 / math.sqrt(head_width)
    far_scores = (
        jnp.einsum("qd,kd->qk", head_queries, keys, preferred_element_type=f32) * inverse_root
    )
    far_max = jnp.max(far_scores, axis=1, keepdims=True)
    far_weights = jnp.exp(far_scores - far_max)
    far_total = jnp.sum(far_weights, axis=1, keepdims=True)
    far_out = jnp.dot(far_weights.astype(bf16), values, preferred_element_type=f32) / far_total
    far_level = far_max + jnp.log(far_total)
    first = far_level.astype(bf16).astype(f32)
    second = (far_level - first).astype(bf16).astype(f32)
    third = far_level - first - second
    lane = lax.broadcasted_iota(jnp.int32, far_out.shape, 1)
    level = jnp.where(lane < 32, first, jnp.where(lane < 64, second, third))
    partial = jnp.concatenate([far_out, level], axis=1).astype(bf16)
    partial, queries, stacked = lax.optimization_barrier((partial, queries, stacked))
    parts = lax.all_to_all(partial.reshape(shards, mine, 2 * head_width), "seq", 0, 0)
    (result_copies,) = call(merge_kernel, [((shards, mine, head_width), bf16)], [], [parts])
    header_all = lax.all_to_all(result_copies, "seq", 0, 0).reshape(
        shards, headers, lines, head_width
    )

    margin_rows = REACH * BLOCK
    extended = jnp.concatenate(
        [
            shift(stacked[rows - margin_rows :], "seq", 1),
            stacked,
            shift(stacked[:margin_rows], "seq", -1),
        ]
    )
    near_keys = extended[:, :head_width]
    near_values = extended[:, head_width:]
    extent = rows + 2 * margin_rows
    key_blocks = seq_place * local_blocks - REACH + jnp.arange(extent, dtype=jnp.int32) // BLOCK
    query_blocks = seq_place * local_blocks + jnp.arange(rows, dtype=jnp.int32) // BLOCK
    limits = jnp.repeat(block_reach, BLOCK)
    key_header = jnp.any(header_ids[:, None] == key_blocks[None, :], axis=0)
    allowed = (key_blocks >= 0)[None, :] & (key_blocks < total_blocks)[None, :]
    allowed = allowed & (jnp.abs(key_blocks[None, :] - query_blocks[:, None]) <= limits[:, None])
    allowed = allowed & jnp.logical_not(key_header)[None, :]
    near_scores = (
        jnp.einsum("qd,kd->qk", queries, near_keys, preferred_element_type=f32) * inverse_root
    )
    near_scores = jnp.where(allowed, near_scores, -jnp.inf)
    head_scores = (
        jnp.einsum("qd,kd->qk", queries, head_keys, preferred_element_type=f32) * inverse_root
    )
    scores = jnp.concatenate([near_scores, head_scores], axis=1)
    row_top = jnp.max(scores, axis=1)
    weights = jnp.exp(scores - row_top[:, None])
    row_sums = jnp.sum(weights, axis=1)
    joined = jnp.concatenate([near_values, head_values], axis=0)
    mixed = (
        jnp.dot(weights.astype(bf16), joined, preferred_element_type=f32) / row_sums[:, None]
    ).astype(bf16)

    blocks = []
    for b in range(local_blocks):
        block = mixed[b * BLOCK : (b + 1) * BLOCK]
        for h in range(headers):
            here = header_ids[h] == seq_place * local_blocks + b
            block = jnp.where(here, header_all[:, h].reshape(BLOCK, head_width), block)
        blocks.append(block)
    attended = jnp.concatenate(blocks, axis=0)
    gathered = lax.all_gather(attended, "section", axis=1, tiled=True)
    return jnp.dot(gathered, output_weight, preferred_element_type=f32).astype(bf16)


def solution(mesh):
    return jax.shard_map(
        on_device,
        mesh=mesh,
        in_specs=(
            P("seq", "section"),
            P("section"),
            P(None, "section"),
            P("section", None),
            P("section", None),
            P(None, "section"),
            P("seq"),
            P(),
        ),
        out_specs=P("seq", "section"),
        check_vma=False,
    )
```

```python
import functools
import math

import jax
import jax.numpy as jnp
from jax import lax
from jax.experimental import pallas as pl
from jax.experimental.pallas import tpu as pltpu
from jax.sharding import PartitionSpec as P

BLOCK = 128
REACH = 2

EPSILON = 1e-05
THETA = 500000.0


def shift(value, axis, by):
    count = lax.axis_size(axis)
    return lax.ppermute(value, axis, [(i, (i + by) % count) for i in range(count)])


def tables(positions, head_width):
    middle = head_width // 2
    frequency = jnp.exp(
        -(2.0 / head_width) * math.log(THETA) * jnp.arange(middle, dtype=jnp.float32)
    )
    angles = positions.astype(jnp.float32)[:, None] * frequency[None, :]
    cosine, sine = jnp.cos(angles), jnp.sin(angles)
    return jnp.concatenate([cosine, cosine], axis=1), jnp.concatenate([-sine, sine], axis=1)

BF16, F32 = jnp.bfloat16, jnp.float32
VMEM_LIMIT = 48 * 1024 * 1024


def call(kernel, outs, scalars, arrays, scratch=(), blocks=None, aliases=None, anywhere=(), flops=None):
    whole = pl.BlockSpec(memory_space=pltpu.VMEM)
    specs = [pl.BlockSpec(memory_space=pltpu.SMEM)] * len(scalars)
    specs += [
        pl.BlockSpec(memory_space=pl.ANY) if i in anywhere else whole for i in range(len(arrays))
    ]
    out_specs = [pl.BlockSpec(memory_space=pl.ANY) if aliases else whole for _ in outs]
    return pl.pallas_call(
        kernel,
        out_shape=[jax.ShapeDtypeStruct(shape, dtype) for shape, dtype in outs],
        in_specs=specs,
        out_specs=out_specs,
        scratch_shapes=list(scratch),
        input_output_aliases=aliases or {},
        compiler_params=pltpu.CompilerParams(vmem_limit_bytes=VMEM_LIMIT),
        cost_estimate=flops
        and pl.CostEstimate(flops=flops, bytes_accessed=0, transcendentals=0),
    )(*scalars, *arrays)


def turn(values, cosine, signed_sine):
    return values * cosine + pltpu.roll(values, values.shape[1] // 2, axis=1) * signed_sine


def spread_down(row, size):
    return jnp.transpose(jnp.broadcast_to(row, (size, size)))


def outgoing_kernel(
    sections, place, header_ids, x, gain, query_weight, key_weight, value_weight, *refs
):
    outs, (picked, keyval_own, squares_own, keyval, rows16) = (
        refs[: sections - 1],
        refs[sections - 1 :],
    )
    rows, part = x.shape
    size = BLOCK
    count = rows // size
    for h in range(picked.shape[0]):
        slot = lax.rem(header_ids[h], count)
        picked[h] = x[pl.ds(pl.multiple_of(slot * size, size), size), :]
    keyval_weight = jnp.concatenate([key_weight[...], value_weight[...]], axis=1)
    rows16[...] = jnp.zeros_like(rows16)
    squares_own[...] = jnp.zeros_like(squares_own)
    for b in range(count):
        block = x[b * size : (b + 1) * size, :].astype(F32)
        total = jnp.sum(block * block, axis=1, keepdims=True)
        line = jnp.transpose(jnp.broadcast_to(total, (size, size)))[0:1, :]
        high = line.astype(BF16).astype(F32)
        squares_own[b : b + 1, :] = line
        rows16[b : b + 1, :] = high
        rows16[count + b : count + b + 1, :] = line - high
        block = block * gain[...]
        high = block.astype(BF16)
        low = (block - high.astype(F32)).astype(BF16)
        both = jnp.dot(
            jnp.concatenate([high, low], axis=0), keyval_weight, preferred_element_type=F32
        )
        keyval[b * size : (b + 1) * size, :] = both[:size] + both[size:]
    here = place[0]
    keyval_own[...] = keyval[pl.ds(pl.multiple_of(here * size, size), size), :]
    width = keyval.shape[1] // 2
    for k in range(1, sections):
        target = lax.rem(here + k, sections)
        out = outs[k - 1]
        out[0:part, :] = query_weight[pl.ds(pl.multiple_of(target * part, part), part), :]
        block = keyval[pl.ds(pl.multiple_of(target * size, size), size), :].astype(BF16)
        out[part : part + size, :] = block[:, :width]
        out[part + size : part + 2 * size, :] = block[:, width:]
        out[part + 2 * size : part + 2 * size + 16, :] = rows16[...].astype(BF16)


def partial_kernel(
    sections, place, x, gain, query_weight, keyval_own, squares_own, cosine, sine, *refs
):
    arrived, (out, squares, normed) = refs[: sections - 1], refs[sections - 1 :]
    rows, part = x.shape
    size = BLOCK
    count = rows // size
    here = place[0]
    total = squares_own[0:count, :]
    keyval = keyval_own[...]
    for piece in arrived:
        tail = piece[part + 2 * size : part + 2 * size + 16, :].astype(F32)
        total = total + tail[0:count, :] + tail[count : 2 * count, :]
        keyval = keyval + jnp.concatenate(
            [
                piece[part : part + size, :].astype(F32),
                piece[part + size : part + 2 * size, :].astype(F32),
            ],
            axis=1,
        )
    squares[0:count, :] = lax.rsqrt(total / (part * sections) + EPSILON)
    for b in range(count):
        scale = spread_down(squares[b : b + 1, :], size)
        scale = jnp.concatenate([scale] * (part // size), axis=1)
        block = x[b * size : (b + 1) * size, :].astype(F32) * scale * gain[...]
        normed[b * size : (b + 1) * size, :] = block.astype(BF16)
    weights = [query_weight[pl.ds(pl.multiple_of(here * part, part), part), :]]
    weights += [piece[0:part, :] for piece in arrived]
    head_width = query_weight.shape[1]
    for k in range(0, sections, 2):
        pair = jnp.concatenate(weights[k : k + 2], axis=1)
        value = jnp.dot(normed[...], pair, preferred_element_type=F32).astype(BF16)
        for j in range(2):
            target = lax.rem(here - k - j + sections, sections)
            out[target, 0:rows, :] = value[:, j * head_width : (j + 1) * head_width]
    scale = spread_down(squares[pl.ds(here, 1), :], size)
    keys = turn(keyval[:, :head_width] * scale, cosine[...], sine[...]).astype(BF16)
    values = (keyval[:, head_width:] * scale).astype(BF16)
    for target in range(sections):
        out[target, rows : rows + size, :] = keys
        out[target, rows + size : rows + 2 * size, :] = values
        out[target, rows + 2 * size : rows + 2 * size + 16, :] = jnp.zeros(
            (16, head_width), BF16
        )


def header_kernel(
    sections,
    offset,
    local_blocks,
    place,
    header_ids,
    spread,
    gain,
    query_weight,
    key_weight,
    value_weight,
    *refs,
):
    arrived, (_, out, small, semaphore) = refs[: sections - 1], refs[sections - 1 :]
    part = gain.shape[1]
    head_width = query_weight.shape[1]
    here = place[0]
    row = lax.broadcasted_iota(jnp.int32, (16, part), 0)
    pair = [spread[lax.div(header_ids[h], local_blocks)].astype(F32) for h in range(2)]
    line = jnp.where(lax.rem(row, 2) == 0, pair[0][0:1, :], pair[1][1:2, :])
    gained = line * gain[...]
    high = gained.astype(BF16)
    low = (gained - high.astype(F32)).astype(BF16)
    left = jnp.concatenate([high, low], axis=0)
    squares = jnp.broadcast_to(jnp.sum(line * line, axis=1, keepdims=True), (16, head_width))
    row = lax.broadcasted_iota(jnp.int32, (16, head_width), 0)

    def product(weight):
        both = jnp.dot(left, weight, preferred_element_type=F32)
        return both[:16] + both[16:]

    keyval = product(jnp.concatenate([key_weight[...], value_weight[...]], axis=1))
    weights = [query_weight[pl.ds(pl.multiple_of(here * part, part), part), :]]
    weights += [piece[0:part, :] for piece in arrived]
    for k in range(0, sections, 2):
        queries = product(jnp.concatenate(weights[k : k + 2], axis=1))
        for j in range(2):
            target = lax.rem(here - k - j + sections, sections)
            value = jnp.where(
                row < 4,
                queries[:, j * head_width : (j + 1) * head_width],
                jnp.where(
                    row < 8,
                    keyval[:, :head_width],
                    jnp.where(row < 12, keyval[:, head_width:], squares),
                ),
            )
            high = value.astype(BF16).astype(F32)
            value = jnp.where(lax.rem(row, 4) < 2, high, value - high)
            small[target] = value.astype(BF16)
    copy = pltpu.make_async_copy(small, out.at[:, pl.ds(offset, 16), :], semaphore)
    copy.start()
    copy.wait()


def header_finish_kernel(width, arrived, cosine, sine, out):
    total = jnp.sum(arrived[...].astype(F32), axis=0)
    total = total + pltpu.roll(total, 14, axis=0)
    scale = lax.rsqrt(pltpu.roll(total, 4, axis=0) / width + EPSILON)
    queries = turn(total * scale, cosine[...], sine[...])
    keys = turn(pltpu.roll(total, 12, axis=0) * scale, cosine[...], sine[...])
    values = pltpu.roll(total, 8, axis=0) * scale
    chunk = jnp.concatenate([queries, keys, values], axis=1)[0:2, :].astype(BF16)
    out[...] = jnp.broadcast_to(chunk[None], out.shape)


def main_finish_kernel(arrived, cosine, sine, queries, keyval):
    rows, head_width = queries.shape
    size = BLOCK
    for b in range(rows // size):
        part = slice(b * size, (b + 1) * size)
        total = jnp.sum(arrived[:, part, :].astype(F32), axis=0)
        queries[part, :] = turn(total, cosine[part, :], sine[part, :]).astype(BF16)
        keyval[part, 0:head_width] = arrived[b, rows : rows + size, :]
        keyval[part, head_width:] = arrived[b, rows + size : rows + 2 * size, :]


def window_kernel(
    total_blocks, seq_place, reach, header_ids, queries, before, here, after, header, out
):
    rows, head_width = queries.shape
    size = BLOCK
    count = rows // size
    parts = [before[j * size : (j + 1) * size, :] for j in range(REACH)]
    parts += [here[j * size : (j + 1) * size, :] for j in range(count)]
    parts += [after[j * size : (j + 1) * size, :] for j in range(REACH)]
    head_keys = header[:, head_width : 2 * head_width]
    head_values = header[:, 2 * head_width :]
    for b in range(count):
        near = parts[b : b + 2 * REACH + 1]
        keys = jnp.concatenate([part[:, :head_width] for part in near] + [head_keys], axis=0)
        values = jnp.concatenate([part[:, head_width:] for part in near] + [head_values], axis=0)
        scores = lax.dot_general(
            queries[b * size : (b + 1) * size, :],
            keys,
            (((1,), (1,)), ((), ())),
            preferred_element_type=F32,
        ) * (1.0 / math.sqrt(head_width))
        pieces = []
        for j in range(2 * REACH + 1):
            block = seq_place[0] * count + b + j - REACH
            allowed = (block >= 0) & (block < total_blocks) & (abs(j - REACH) <= reach[b])
            for h in range(2):
                allowed = allowed & (block != header_ids[h])
            pieces.append(
                jnp.where(allowed, scores[:, j * size : (j + 1) * size], -jnp.inf)
            )
        pieces.append(scores[:, (2 * REACH + 1) * size :])
        scores = jnp.concatenate(pieces, axis=1)
        weights = jnp.exp(scores - jnp.max(scores, axis=1, keepdims=True))
        total = jnp.sum(weights, axis=1, keepdims=True)
        mixed = jnp.dot(weights.astype(BF16), values, preferred_element_type=F32)
        out[b * size : (b + 1) * size, :] = (mixed / total).astype(BF16)


def merge_kernel(parts, out):
    head_width = out.shape[2]
    everything = parts[...].astype(F32)
    level = everything[:, :, head_width:]
    level = level[:, :, 0:1] + level[:, :, 32:33] + level[:, :, 64:65]
    factor = jnp.exp(level - jnp.max(level, axis=0, keepdims=True))
    total = jnp.sum(everything[:, :, :head_width] * factor, axis=0)
    result = (total / jnp.sum(factor, axis=0)).astype(BF16)
    out[...] = jnp.broadcast_to(result[None], out.shape)


def on_device(
    hidden,
    norm_gain,
    query_weight,
    key_weight,
    value_weight,
    output_weight,
    block_reach,
    header_ids,
):
    bf16, f32 = jnp.bfloat16, jnp.float32
    rows, part = hidden.shape
    head_width = key_weight.shape[1]
    sections = lax.axis_size("section")
    shards = lax.axis_size("seq")
    local_blocks = rows // BLOCK
    total_blocks = local_blocks * shards
    section_place = lax.axis_index("section")
    seq_place = lax.axis_index("seq")
    headers = header_ids.shape[0]
    lines = BLOCK // shards
    mine = headers * lines
    width = part * sections
    gain = norm_gain.astype(f32)[None, :]

    place = section_place.astype(jnp.int32).reshape(1)
    tall = part + 2 * BLOCK + 16
    *outgoing, picked, keyval_own, squares_own = call(
        functools.partial(outgoing_kernel, sections),
        [((tall, head_width), bf16)] * (sections - 1)
        + [
            ((headers, BLOCK, part), bf16),
            ((BLOCK, 2 * head_width), f32),
            ((8, head_width), f32),
        ],
        [place, header_ids],
        [hidden, gain, query_weight, key_weight, value_weight],
        [pltpu.VMEM((rows, 2 * head_width), f32), pltpu.VMEM((16, head_width), f32)],
    )
    spread = lax.all_to_all(picked.transpose(1, 0, 2), "seq", 0, 0)
    incoming = [shift(outgoing[k - 1], "section", k) for k in range(1, sections)]
    own_positions = seq_place * rows + jnp.arange(rows, dtype=jnp.int32)
    own_tables = tables(own_positions, head_width)
    block_tables = [
        lax.dynamic_slice_in_dim(table, section_place * BLOCK, BLOCK, axis=0)
        for table in own_tables
    ]
    length = rows + 2 * BLOCK + 16
    (payload,) = call(
        functools.partial(partial_kernel, sections),
        [((sections, length, head_width), bf16)],
        [place],
        [hidden, gain, query_weight, keyval_own, squares_own, *block_tables, *incoming],
        [pltpu.VMEM((8, head_width), f32), pltpu.VMEM((rows, part), bf16)],
        flops=10**11,
    )
    (payload,) = call(
        functools.partial(header_kernel, sections, length - 16, local_blocks),
        [((sections, length, head_width), bf16)],
        [place, header_ids],
        [spread, gain, query_weight, key_weight, value_weight, *incoming, payload],
        [pltpu.VMEM((sections, 16, head_width), bf16), pltpu.SemaphoreType.DMA],
        aliases={6 + sections: 0},
        anywhere=(4 + sections,),
    )
    arrived = lax.all_to_all(payload, "section", 0, 0)

    index = jnp.arange(16, dtype=jnp.int32) % 2
    header_positions = jnp.where(index == 0, header_ids[0], header_ids[1]) * BLOCK + seq_place
    (header_copies,) = call(
        functools.partial(header_finish_kernel, width),
        [((shards, mine, 3 * head_width), bf16)],
        [],
        [arrived[:, length - 16 :], *tables(header_positions, head_width)],
    )
    header_pack = lax.all_to_all(header_copies, "seq", 0, 0).reshape(-1, 3 * head_width)
    queries, stacked = call(
        main_finish_kernel,
        [((rows, head_width), bf16), ((rows, 2 * head_width), bf16)],
        [],
        [arrived, *own_tables],
    )
    keys, values = stacked[:, :head_width], stacked[:, head_width:]
    head_queries = header_pack[:, :head_width]
    head_keys = header_pack[:, head_width : 2 * head_width]
    head_values = header_pack[:, 2 * head_width :]

    inverse_root = 1.0 / math.sqrt(head_width)
    far_scores = (
        jnp.einsum("qd,kd->qk", head_queries, keys, preferred_element_type=f32) * inverse_root
    )
    far_max = jnp.max(far_scores, axis=1, keepdims=True)
    far_weights = jnp.exp(far_scores - far_max)
    far_total = jnp.sum(far_weights, axis=1, keepdims=True)
    far_out = jnp.dot(far_weights.astype(bf16), values, preferred_element_type=f32) / far_total
    far_level = far_max + jnp.log(far_total)
    first = far_level.astype(bf16).astype(f32)
    second = (far_level - first).astype(bf16).astype(f32)
    third = far_level - first - second
    lane = lax.broadcasted_iota(jnp.int32, far_out.shape, 1)
    level = jnp.where(lane < 32, first, jnp.where(lane < 64, second, third))
    partial = jnp.concatenate([far_out, level], axis=1).astype(bf16)
    partial, queries, stacked = lax.optimization_barrier((partial, queries, stacked))
    margin_rows = REACH * BLOCK
    parts = lax.all_to_all(partial.reshape(shards, mine, 2 * head_width), "seq", 0, 0)
    (result_copies,) = call(merge_kernel, [((shards, mine, head_width), bf16)], [], [parts])
    before, after = shift(stacked[rows - margin_rows :], "seq", 1), shift(
        stacked[:margin_rows], "seq", -1
    )
    result_copies, queries = lax.optimization_barrier((result_copies, queries))
    header_all = lax.all_to_all(result_copies, "seq", 0, 0).reshape(
        shards, headers, lines, head_width
    )

    (mixed,) = call(
        functools.partial(window_kernel, total_blocks),
        [((rows, head_width), bf16)],
        [seq_place.astype(jnp.int32).reshape(1), block_reach, header_ids],
        [queries, before, stacked, after, header_pack],
    )

    blocks = []
    for b in range(local_blocks):
        block = mixed[b * BLOCK : (b + 1) * BLOCK]
        for h in range(headers):
            here = header_ids[h] == seq_place * local_blocks + b
            block = jnp.where(here, header_all[:, h].reshape(BLOCK, head_width), block)
        blocks.append(block)
    attended = jnp.concatenate(blocks, axis=0)
    gathered = lax.all_gather(attended, "section", axis=1, tiled=True)
    return jnp.dot(gathered, output_weight, preferred_element_type=f32).astype(bf16)


def solution(mesh):
    return jax.shard_map(
        on_device,
        mesh=mesh,
        in_specs=(
            P("seq", "section"),
            P("section"),
            P(None, "section"),
            P("section", None),
            P("section", None),
            P(None, "section"),
            P("seq"),
            P(),
        ),
        out_specs=P("seq", "section"),
        check_vma=False,
    )
```

```python
import functools
import math

import jax
import jax.numpy as jnp
from jax import lax
from jax.experimental import pallas as pl
from jax.experimental.pallas import tpu as pltpu
from jax.sharding import PartitionSpec as P

BLOCK = 128
REACH = 2

EPSILON = 1e-05
THETA = 500000.0


def shift(value, axis, by):
    count = lax.axis_size(axis)
    return lax.ppermute(value, axis, [(i, (i + by) % count) for i in range(count)])


def tables(positions, head_width):
    middle = head_width // 2
    frequency = jnp.exp(
        -(2.0 / head_width) * math.log(THETA) * jnp.arange(middle, dtype=jnp.float32)
    )
    angles = positions.astype(jnp.float32)[:, None] * frequency[None, :]
    cosine, sine = jnp.cos(angles), jnp.sin(angles)
    return jnp.concatenate([cosine, cosine], axis=1), jnp.concatenate([-sine, sine], axis=1)

BF16, F32 = jnp.bfloat16, jnp.float32
VMEM_LIMIT = 24 * 1024 * 1024


def call(kernel, outs, scalars, arrays, scratch=()):
    whole = pl.BlockSpec(memory_space=pltpu.VMEM)
    specs = [pl.BlockSpec(memory_space=pltpu.SMEM)] * len(scalars)
    specs += [whole] * len(arrays)
    return pl.pallas_call(
        kernel,
        out_shape=[jax.ShapeDtypeStruct(shape, dtype) for shape, dtype in outs],
        in_specs=specs,
        out_specs=[whole] * len(outs),
        scratch_shapes=list(scratch),
        compiler_params=pltpu.CompilerParams(vmem_limit_bytes=VMEM_LIMIT),
    )(*scalars, *arrays)


def turn(values, cosine, signed_sine):
    return values * cosine + pltpu.roll(values, values.shape[1] // 2, axis=1) * signed_sine


def spread_down(row, size):
    return jnp.transpose(jnp.broadcast_to(row, (size, size)))


def outgoing_kernel(sections, x, gain, query_weight, key_weight, value_weight, out, keyval, rows16):
    rows, part = x.shape
    size = BLOCK
    count = rows // size
    keyval_weight = jnp.concatenate([key_weight[...], value_weight[...]], axis=1)
    rows16[...] = jnp.zeros_like(rows16)
    for b in range(count):
        block = x[b * size : (b + 1) * size, :].astype(F32)
        total = jnp.sum(block * block, axis=1, keepdims=True)
        line = jnp.transpose(jnp.broadcast_to(total, (size, size)))[0:1, :]
        high = line.astype(BF16).astype(F32)
        rows16[b : b + 1, :] = high
        rows16[count + b : count + b + 1, :] = line - high
        block = block * gain[...]
        high = block.astype(BF16)
        low = (block - high.astype(F32)).astype(BF16)
        both = jnp.dot(
            jnp.concatenate([high, low], axis=0), keyval_weight, preferred_element_type=F32
        )
        keyval[b * size : (b + 1) * size, :] = (both[:size] + both[size:]).astype(BF16)
    width = keyval.shape[1] // 2
    for target in range(sections):
        out[target, 0:part, :] = query_weight[target * part : (target + 1) * part, :]
        block = keyval[target * size : (target + 1) * size, :]
        out[target, part : part + size, :] = block[:, :width]
        out[target, part + size : part + 2 * size, :] = block[:, width:]
        out[target, part + 2 * size : part + 2 * size + 16, :] = rows16[...].astype(BF16)


def partial_kernel(sections, place, x, gain, arrived, cosine, sine, out, squares, normed):
    rows, part = x.shape
    size = BLOCK
    count = rows // size
    head_width = arrived.shape[2]
    tail = jnp.sum(arrived[:, part + 2 * size : part + 2 * size + 16, :].astype(F32), axis=0)
    squares[0:count, :] = lax.rsqrt(
        (tail[0:count, :] + tail[count : 2 * count, :]) / (part * sections) + EPSILON
    )
    for b in range(count):
        scale = spread_down(squares[b : b + 1, :], size)
        scale = jnp.concatenate([scale] * (part // size), axis=1)
        block = x[b * size : (b + 1) * size, :].astype(F32) * scale * gain[...]
        normed[b * size : (b + 1) * size, :] = block.astype(BF16)
    for k in range(0, sections, 2):
        pair = jnp.concatenate([arrived[k, 0:part, :], arrived[k + 1, 0:part, :]], axis=1)
        value = jnp.dot(normed[...], pair, preferred_element_type=F32).astype(BF16)
        out[k, 0:rows, :] = value[:, :head_width]
        out[k + 1, 0:rows, :] = value[:, head_width:]
    scale = spread_down(squares[pl.ds(place[0], 1), :], size)
    keys = jnp.sum(arrived[:, part : part + size, :].astype(F32), axis=0)
    keys = turn(keys * scale, cosine[...], sine[...]).astype(BF16)
    values = jnp.sum(arrived[:, part + size : part + 2 * size, :].astype(F32), axis=0)
    values = (values * scale).astype(BF16)
    for target in range(sections):
        out[target, rows : rows + size, :] = keys
        out[target, rows + size : rows + 2 * size, :] = values


def finish_kernel(header_ids, arrived, cosine, sine, queries, keyval, picked):
    rows, head_width = queries.shape
    size = BLOCK
    count = rows // size
    for b in range(count):
        part = slice(b * size, (b + 1) * size)
        total = jnp.sum(arrived[:, part, :].astype(F32), axis=0)
        queries[part, :] = turn(total, cosine[part, :], sine[part, :]).astype(BF16)
        keyval[part, 0:head_width] = arrived[b, rows : rows + size, :]
        keyval[part, head_width:] = arrived[b, rows + size : rows + 2 * size, :]
    for h in range(picked.shape[0] // size):
        start = pl.multiple_of(lax.rem(header_ids[h], count) * size, size)
        picked[h * size : (h + 1) * size, 0:head_width] = queries[pl.ds(start, size), :]
        picked[h * size : (h + 1) * size, head_width:] = keyval[pl.ds(start, size), :]


def repeat_kernel(seq_place, header_ids, local_blocks, spread, out):
    header = lax.div(seq_place[0] * spread.shape[1], BLOCK)
    rows = spread[lax.div(header_ids[header], local_blocks[0])]
    out[...] = jnp.broadcast_to(rows[None], out.shape)


def window_kernel(
    total_blocks, seq_place, reach, header_ids, queries, before, here, after, header, out
):
    rows, head_width = queries.shape
    size = BLOCK
    count = rows // size
    parts = [before[j * size : (j + 1) * size, :] for j in range(REACH)]
    parts += [here[j * size : (j + 1) * size, :] for j in range(count)]
    parts += [after[j * size : (j + 1) * size, :] for j in range(REACH)]
    head_keys = header[:, head_width : 2 * head_width]
    head_values = header[:, 2 * head_width :]
    for b in range(count):
        near = parts[b : b + 2 * REACH + 1]
        keys = jnp.concatenate([part[:, :head_width] for part in near] + [head_keys], axis=0)
        values = jnp.concatenate([part[:, head_width:] for part in near] + [head_values], axis=0)
        scores = lax.dot_general(
            queries[b * size : (b + 1) * size, :],
            keys,
            (((1,), (1,)), ((), ())),
            preferred_element_type=F32,
        ) * (1.0 / math.sqrt(head_width))
        pieces = []
        for j in range(2 * REACH + 1):
            block = seq_place[0] * count + b + j - REACH
            allowed = (block >= 0) & (block < total_blocks) & (abs(j - REACH) <= reach[b])
            for h in range(2):
                allowed = allowed & (block != header_ids[h])
            pieces.append(
                jnp.where(allowed, scores[:, j * size : (j + 1) * size], -jnp.inf)
            )
        pieces.append(scores[:, (2 * REACH + 1) * size :])
        scores = jnp.concatenate(pieces, axis=1)
        weights = jnp.exp(scores - jnp.max(scores, axis=1, keepdims=True))
        total = jnp.sum(weights, axis=1, keepdims=True)
        mixed = jnp.dot(weights.astype(BF16), values, preferred_element_type=F32)
        out[b * size : (b + 1) * size, :] = (mixed / total).astype(BF16)


def merge_kernel(parts, out):
    head_width = out.shape[2]
    everything = parts[...].astype(F32)
    level = everything[:, :, head_width:]
    level = level[:, :, 0:1] + level[:, :, 32:33] + level[:, :, 64:65]
    factor = jnp.exp(level - jnp.max(level, axis=0, keepdims=True))
    total = jnp.sum(everything[:, :, :head_width] * factor, axis=0)
    result = (total / jnp.sum(factor, axis=0)).astype(BF16)
    out[...] = jnp.broadcast_to(result[None], out.shape)


def on_device(
    hidden,
    norm_gain,
    query_weight,
    key_weight,
    value_weight,
    output_weight,
    block_reach,
    header_ids,
):
    bf16, f32 = jnp.bfloat16, jnp.float32
    rows, part = hidden.shape
    head_width = key_weight.shape[1]
    sections = lax.axis_size("section")
    shards = lax.axis_size("seq")
    local_blocks = rows // BLOCK
    total_blocks = local_blocks * shards
    section_place = lax.axis_index("section")
    seq_place = lax.axis_index("seq")
    headers = header_ids.shape[0]
    mine = headers * BLOCK // shards
    gain = norm_gain.astype(f32)[None, :]

    places = [place.astype(jnp.int32).reshape(1) for place in (section_place, seq_place)]
    tall = part + 2 * BLOCK + 16
    (outgoing,) = call(
        functools.partial(outgoing_kernel, sections),
        [((sections, tall, head_width), bf16)],
        [],
        [hidden, gain, query_weight, key_weight, value_weight],
        [pltpu.VMEM((rows, 2 * head_width), bf16), pltpu.VMEM((16, head_width), f32)],
    )
    incoming = lax.all_to_all(outgoing, "section", 0, 0)
    own_positions = seq_place * rows + jnp.arange(rows, dtype=jnp.int32)
    own_tables = tables(own_positions, head_width)
    block_tables = [
        lax.dynamic_slice_in_dim(table, section_place * BLOCK, BLOCK, axis=0)
        for table in own_tables
    ]
    (payload,) = call(
        functools.partial(partial_kernel, sections),
        [((sections, rows + 2 * BLOCK, head_width), bf16)],
        [places[0]],
        [hidden, gain, incoming, *block_tables],
        [pltpu.VMEM((8, head_width), f32), pltpu.VMEM((rows, part), bf16)],
    )
    arrived = lax.all_to_all(payload, "section", 0, 0)
    queries, stacked, picked = call(
        finish_kernel,
        [
            ((rows, head_width), bf16),
            ((rows, 2 * head_width), bf16),
            ((headers * BLOCK, 3 * head_width), bf16),
        ],
        [header_ids],
        [arrived, *own_tables],
    )

    spread = lax.all_to_all(picked.reshape(shards, mine, 3 * head_width), "seq", 0, 0)
    (header_copies,) = call(
        repeat_kernel,
        [((shards, mine, 3 * head_width), bf16)],
        [places[1], header_ids, jnp.full((1,), local_blocks, jnp.int32)],
        [spread],
    )
    header_copies, edges = lax.optimization_barrier((header_copies, stacked))
    header_pack = lax.all_to_all(header_copies, "seq", 0, 0).reshape(-1, 3 * head_width)
    margin_rows = REACH * BLOCK
    before = shift(edges[rows - margin_rows :], "seq", 1)
    after = shift(edges[:margin_rows], "seq", -1)
    keys, values = stacked[:, :head_width], stacked[:, head_width:]
    head_queries = header_pack[:, :head_width]
    head_keys = header_pack[:, head_width : 2 * head_width]
    head_values = header_pack[:, 2 * head_width :]

    inverse_root = 1.0 / math.sqrt(head_width)
    far_scores = (
        jnp.einsum("qd,kd->qk", head_queries, keys, preferred_element_type=f32) * inverse_root
    )
    far_max = jnp.max(far_scores, axis=1, keepdims=True)
    far_weights = jnp.exp(far_scores - far_max)
    far_total = jnp.sum(far_weights, axis=1, keepdims=True)
    far_out = jnp.dot(far_weights.astype(bf16), values, preferred_element_type=f32) / far_total
    far_level = far_max + jnp.log(far_total)
    first = far_level.astype(bf16).astype(f32)
    second = (far_level - first).astype(bf16).astype(f32)
    third = far_level - first - second
    lane = lax.broadcasted_iota(jnp.int32, far_out.shape, 1)
    level = jnp.where(lane < 32, first, jnp.where(lane < 64, second, third))
    partial = jnp.concatenate([far_out, level], axis=1).astype(bf16)
    partial, queries = lax.optimization_barrier((partial, queries))
    parts = lax.all_to_all(partial.reshape(shards, mine, 2 * head_width), "seq", 0, 0)
    (result_copies,) = call(merge_kernel, [((shards, mine, head_width), bf16)], [], [parts])
    header_all = lax.all_to_all(result_copies, "seq", 0, 0).reshape(
        headers, BLOCK, head_width
    )

    (mixed,) = call(
        functools.partial(window_kernel, total_blocks),
        [((rows, head_width), bf16)],
        [places[1], block_reach, header_ids],
        [queries, before, stacked, after, header_pack],
    )

    blocks = []
    for b in range(local_blocks):
        block = mixed[b * BLOCK : (b + 1) * BLOCK]
        for h in range(headers):
            here = header_ids[h] == seq_place * local_blocks + b
            block = jnp.where(here, header_all[h], block)
        blocks.append(block)
    attended = jnp.concatenate(blocks, axis=0)
    gathered = lax.all_gather(attended, "section", axis=1, tiled=True)
    return jnp.dot(gathered, output_weight, preferred_element_type=f32).astype(bf16)


def solution(mesh):
    return jax.shard_map(
        on_device,
        mesh=mesh,
        in_specs=(
            P("seq", "section"),
            P("section"),
            P(None, "section"),
            P("section", None),
            P("section", None),
            P(None, "section"),
            P("seq"),
            P(),
        ),
        out_specs=P("seq", "section"),
        check_vma=False,
    )
```

```python
import functools
import math

import jax
import jax.numpy as jnp
from jax import lax
from jax.experimental import pallas as pl
from jax.experimental.pallas import tpu as pltpu
from jax.sharding import PartitionSpec as P

BLOCK = 128
REACH = 2

EPSILON = 1e-05
THETA = 500000.0


def shift(value, axis, by):
    count = lax.axis_size(axis)
    return lax.ppermute(value, axis, [(i, (i + by) % count) for i in range(count)])


def tables(positions, head_width):
    middle = head_width // 2
    frequency = jnp.exp(
        -(2.0 / head_width) * math.log(THETA) * jnp.arange(middle, dtype=jnp.float32)
    )
    angles = positions.astype(jnp.float32)[:, None] * frequency[None, :]
    cosine, sine = jnp.cos(angles), jnp.sin(angles)
    return jnp.concatenate([cosine, cosine], axis=1), jnp.concatenate([-sine, sine], axis=1)

BF16, F32 = jnp.bfloat16, jnp.float32
VMEM_LIMIT = 24 * 1024 * 1024


def call(kernel, outs, scalars, arrays, scratch=()):
    whole = pl.BlockSpec(memory_space=pltpu.VMEM)
    specs = [pl.BlockSpec(memory_space=pltpu.SMEM)] * len(scalars)
    specs += [whole] * len(arrays)
    return pl.pallas_call(
        kernel,
        out_shape=[jax.ShapeDtypeStruct(shape, dtype) for shape, dtype in outs],
        in_specs=specs,
        out_specs=[whole] * len(outs),
        scratch_shapes=list(scratch),
        compiler_params=pltpu.CompilerParams(vmem_limit_bytes=VMEM_LIMIT),
    )(*scalars, *arrays)


def turn(values, cosine, signed_sine):
    return values * cosine + pltpu.roll(values, values.shape[1] // 2, axis=1) * signed_sine


def spread_down(row, size):
    return jnp.transpose(jnp.broadcast_to(row, (size, size)))


def outgoing_kernel(sections, x, gain, query_weight, key_weight, value_weight, out, keyval, rows16):
    rows, part = x.shape
    size = BLOCK
    count = rows // size
    keyval_weight = jnp.concatenate([key_weight[...], value_weight[...]], axis=1)
    rows16[...] = jnp.zeros_like(rows16)
    for b in range(count):
        block = x[b * size : (b + 1) * size, :].astype(F32)
        total = jnp.sum(block * block, axis=1, keepdims=True)
        line = jnp.transpose(jnp.broadcast_to(total, (size, size)))[0:1, :]
        high = line.astype(BF16).astype(F32)
        rows16[b : b + 1, :] = high
        rows16[count + b : count + b + 1, :] = line - high
        block = block * gain[...]
        high = block.astype(BF16)
        low = (block - high.astype(F32)).astype(BF16)
        both = jnp.dot(
            jnp.concatenate([high, low], axis=0), keyval_weight, preferred_element_type=F32
        )
        keyval[b * size : (b + 1) * size, :] = (both[:size] + both[size:]).astype(BF16)
    width = keyval.shape[1] // 2
    for target in range(sections):
        out[target, 0:part, :] = query_weight[target * part : (target + 1) * part, :]
        block = keyval[target * size : (target + 1) * size, :]
        out[target, part : part + size, :] = block[:, :width]
        out[target, part + size : part + 2 * size, :] = block[:, width:]
        out[target, part + 2 * size : part + 2 * size + 16, :] = rows16[...].astype(BF16)


def partial_kernel(sections, place, x, gain, arrived, cosine, sine, out, squares, normed):
    rows, part = x.shape
    size = BLOCK
    count = rows // size
    head_width = arrived.shape[2]
    tail = jnp.sum(arrived[:, part + 2 * size : part + 2 * size + 16, :].astype(F32), axis=0)
    squares[0:count, :] = lax.rsqrt(
        (tail[0:count, :] + tail[count : 2 * count, :]) / (part * sections) + EPSILON
    )
    for b in range(count):
        scale = spread_down(squares[b : b + 1, :], size)
        scale = jnp.concatenate([scale] * (part // size), axis=1)
        block = x[b * size : (b + 1) * size, :].astype(F32) * scale * gain[...]
        normed[b * size : (b + 1) * size, :] = block.astype(BF16)
    for k in range(0, sections, 2):
        pair = jnp.concatenate([arrived[k, 0:part, :], arrived[k + 1, 0:part, :]], axis=1)
        value = jnp.dot(normed[...], pair, preferred_element_type=F32).astype(BF16)
        out[k, 0:rows, :] = value[:, :head_width]
        out[k + 1, 0:rows, :] = value[:, head_width:]
    scale = spread_down(squares[pl.ds(place[0], 1), :], size)
    keys = jnp.sum(arrived[:, part : part + size, :].astype(F32), axis=0)
    keys = turn(keys * scale, cosine[...], sine[...]).astype(BF16)
    values = jnp.sum(arrived[:, part + size : part + 2 * size, :].astype(F32), axis=0)
    values = (values * scale).astype(BF16)
    for target in range(sections):
        out[target, rows : rows + size, :] = keys
        out[target, rows + size : rows + 2 * size, :] = values


def finish_kernel(header_ids, arrived, cosine, sine, queries, keyval, picked):
    rows, head_width = queries.shape
    size = BLOCK
    count = rows // size
    for b in range(count):
        part = slice(b * size, (b + 1) * size)
        total = jnp.sum(arrived[:, part, :].astype(F32), axis=0)
        queries[part, :] = turn(total, cosine[part, :], sine[part, :]).astype(BF16)
        keyval[part, 0:head_width] = arrived[b, rows : rows + size, :]
        keyval[part, head_width:] = arrived[b, rows + size : rows + 2 * size, :]
    for h in range(picked.shape[0] // size):
        start = pl.multiple_of(lax.rem(header_ids[h], count) * size, size)
        picked[h * size : (h + 1) * size, 0:head_width] = queries[pl.ds(start, size), :]
        picked[h * size : (h + 1) * size, head_width:] = keyval[pl.ds(start, size), :]


def repeat_kernel(seq_place, header_ids, local_blocks, spread, out):
    header = lax.div(seq_place[0] * spread.shape[1], BLOCK)
    rows = spread[lax.div(header_ids[header], local_blocks[0])]
    out[...] = jnp.broadcast_to(rows[None], out.shape)


def window_kernel(
    total_blocks, seq_place, reach, header_ids, queries, before, here, after, header, out
):
    rows, head_width = queries.shape
    size = BLOCK
    count = rows // size
    parts = [before[j * size : (j + 1) * size, :] for j in range(REACH)]
    parts += [here[j * size : (j + 1) * size, :] for j in range(count)]
    parts += [after[j * size : (j + 1) * size, :] for j in range(REACH)]
    head_keys = header[:, head_width : 2 * head_width]
    head_values = header[:, 2 * head_width :]
    for b in range(count):
        near = parts[b : b + 2 * REACH + 1]
        keys = jnp.concatenate([part[:, :head_width] for part in near] + [head_keys], axis=0)
        values = jnp.concatenate([part[:, head_width:] for part in near] + [head_values], axis=0)
        scores = lax.dot_general(
            queries[b * size : (b + 1) * size, :],
            keys,
            (((1,), (1,)), ((), ())),
            preferred_element_type=F32,
        ) * (1.0 / math.sqrt(head_width))
        pieces = []
        for j in range(2 * REACH + 1):
            block = seq_place[0] * count + b + j - REACH
            allowed = (block >= 0) & (block < total_blocks) & (abs(j - REACH) <= reach[b])
            for h in range(2):
                allowed = allowed & (block != header_ids[h])
            pieces.append(
                jnp.where(allowed, scores[:, j * size : (j + 1) * size], -jnp.inf)
            )
        pieces.append(scores[:, (2 * REACH + 1) * size :])
        scores = jnp.concatenate(pieces, axis=1)
        weights = jnp.exp(scores - jnp.max(scores, axis=1, keepdims=True))
        total = jnp.sum(weights, axis=1, keepdims=True)
        mixed = jnp.dot(weights.astype(BF16), values, preferred_element_type=F32)
        out[b * size : (b + 1) * size, :] = (mixed / total).astype(BF16)


def place_kernel(seq_place, header_ids, attended, weight, _, out, block, semaphore):
    size = BLOCK
    count = out.shape[0] // size
    for h in range(2):

        @pl.when(lax.div(header_ids[h], count) == seq_place[0])
        def _():
            rows = slice(h * size, (h + 1) * size)
            left = jnp.concatenate(
                [attended[s, rows, :] for s in range(attended.shape[0])], axis=1
            )
            block[...] = jnp.dot(left, weight[...], preferred_element_type=F32).astype(BF16)
            start = pl.multiple_of(lax.rem(header_ids[h], count) * size, size)
            copy = pltpu.make_async_copy(block, out.at[pl.ds(start, size), :], semaphore)
            copy.start()
            copy.wait()


def merge_kernel(parts, out):
    head_width = out.shape[2]
    everything = parts[...].astype(F32)
    level = everything[:, :, head_width:]
    level = level[:, :, 0:1] + level[:, :, 32:33] + level[:, :, 64:65]
    factor = jnp.exp(level - jnp.max(level, axis=0, keepdims=True))
    total = jnp.sum(everything[:, :, :head_width] * factor, axis=0)
    result = (total / jnp.sum(factor, axis=0)).astype(BF16)
    out[...] = jnp.broadcast_to(result[None], out.shape)


def on_device(
    hidden,
    norm_gain,
    query_weight,
    key_weight,
    value_weight,
    output_weight,
    block_reach,
    header_ids,
):
    bf16, f32 = jnp.bfloat16, jnp.float32
    rows, part = hidden.shape
    head_width = key_weight.shape[1]
    sections = lax.axis_size("section")
    shards = lax.axis_size("seq")
    local_blocks = rows // BLOCK
    total_blocks = local_blocks * shards
    section_place = lax.axis_index("section")
    seq_place = lax.axis_index("seq")
    headers = header_ids.shape[0]
    mine = headers * BLOCK // shards
    gain = norm_gain.astype(f32)[None, :]

    places = [place.astype(jnp.int32).reshape(1) for place in (section_place, seq_place)]
    tall = part + 2 * BLOCK + 16
    (outgoing,) = call(
        functools.partial(outgoing_kernel, sections),
        [((sections, tall, head_width), bf16)],
        [],
        [hidden, gain, query_weight, key_weight, value_weight],
        [pltpu.VMEM((rows, 2 * head_width), bf16), pltpu.VMEM((16, head_width), f32)],
    )
    incoming = lax.all_to_all(outgoing, "section", 0, 0)
    own_positions = seq_place * rows + jnp.arange(rows, dtype=jnp.int32)
    own_tables = tables(own_positions, head_width)
    block_tables = [
        lax.dynamic_slice_in_dim(table, section_place * BLOCK, BLOCK, axis=0)
        for table in own_tables
    ]
    (payload,) = call(
        functools.partial(partial_kernel, sections),
        [((sections, rows + 2 * BLOCK, head_width), bf16)],
        [places[0]],
        [hidden, gain, incoming, *block_tables],
        [pltpu.VMEM((8, head_width), f32), pltpu.VMEM((rows, part), bf16)],
    )
    arrived = lax.all_to_all(payload, "section", 0, 0)
    queries, stacked, picked = call(
        finish_kernel,
        [
            ((rows, head_width), bf16),
            ((rows, 2 * head_width), bf16),
            ((headers * BLOCK, 3 * head_width), bf16),
        ],
        [header_ids],
        [arrived, *own_tables],
    )

    spread = lax.all_to_all(picked.reshape(shards, mine, 3 * head_width), "seq", 0, 0)
    (header_copies,) = call(
        repeat_kernel,
        [((shards, mine, 3 * head_width), bf16)],
        [places[1], header_ids, jnp.full((1,), local_blocks, jnp.int32)],
        [spread],
    )
    header_copies, edges = lax.optimization_barrier((header_copies, stacked))
    header_pack = lax.all_to_all(header_copies, "seq", 0, 0).reshape(-1, 3 * head_width)
    margin_rows = REACH * BLOCK
    before = shift(edges[rows - margin_rows :], "seq", 1)
    after = shift(edges[:margin_rows], "seq", -1)
    keys, values = stacked[:, :head_width], stacked[:, head_width:]
    head_queries = header_pack[:, :head_width]
    head_keys = header_pack[:, head_width : 2 * head_width]
    head_values = header_pack[:, 2 * head_width :]

    inverse_root = 1.0 / math.sqrt(head_width)
    far_scores = (
        jnp.einsum("qd,kd->qk", head_queries, keys, preferred_element_type=f32) * inverse_root
    )
    far_max = jnp.max(far_scores, axis=1, keepdims=True)
    far_weights = jnp.exp(far_scores - far_max)
    far_total = jnp.sum(far_weights, axis=1, keepdims=True)
    far_out = jnp.dot(far_weights.astype(bf16), values, preferred_element_type=f32) / far_total
    far_level = far_max + jnp.log(far_total)
    first = far_level.astype(bf16).astype(f32)
    second = (far_level - first).astype(bf16).astype(f32)
    third = far_level - first - second
    lane = lax.broadcasted_iota(jnp.int32, far_out.shape, 1)
    level = jnp.where(lane < 32, first, jnp.where(lane < 64, second, third))
    partial = jnp.concatenate([far_out, level], axis=1).astype(bf16)
    partial, queries, before, after = lax.optimization_barrier(
        (partial, queries, before, after)
    )
    parts = lax.all_to_all(partial.reshape(shards, mine, 2 * head_width), "seq", 0, 0)
    everywhere = sections * shards
    (mixed,) = call(
        functools.partial(window_kernel, total_blocks),
        [((rows, head_width), bf16)],
        [places[1], block_reach, header_ids],
        [queries, before, stacked, after, header_pack],
    )
    (result_copies,) = call(
        merge_kernel, [((everywhere, mine, head_width), bf16)], [], [parts]
    )
    result_copies, mixed = lax.optimization_barrier((result_copies, mixed))
    header_all = lax.all_to_all(result_copies, ("section", "seq"), 0, 0).reshape(
        sections, headers * BLOCK, head_width
    )
    gathered = lax.all_gather(mixed, "section", axis=1, tiled=True)
    result = jnp.dot(gathered, output_weight, preferred_element_type=f32).astype(bf16)
    whole = pl.BlockSpec(memory_space=pltpu.VMEM)
    scalar = pl.BlockSpec(memory_space=pltpu.SMEM)
    anywhere = pl.BlockSpec(memory_space=pl.ANY)
    return pl.pallas_call(
        place_kernel,
        out_shape=jax.ShapeDtypeStruct(result.shape, bf16),
        in_specs=[scalar, scalar, whole, whole, anywhere],
        out_specs=anywhere,
        scratch_shapes=[pltpu.VMEM((BLOCK, result.shape[1]), bf16), pltpu.SemaphoreType.DMA],
        input_output_aliases={4: 0},
        compiler_params=pltpu.CompilerParams(vmem_limit_bytes=VMEM_LIMIT),
    )(places[1], header_ids, header_all, output_weight, result)


def solution(mesh):
    return jax.shard_map(
        on_device,
        mesh=mesh,
        in_specs=(
            P("seq", "section"),
            P("section"),
            P(None, "section"),
            P("section", None),
            P("section", None),
            P(None, "section"),
            P("seq"),
            P(),
        ),
        out_specs=P("seq", "section"),
        check_vma=False,
    )
```

```python
import functools
import math

import jax
import jax.numpy as jnp
from jax import lax
from jax.experimental import pallas as pl
from jax.experimental.pallas import tpu as pltpu
from jax.sharding import PartitionSpec as P

BLOCK = 128
REACH = 2

EPSILON = 1e-05
THETA = 500000.0


def shift(value, axis, by):
    count = lax.axis_size(axis)
    return lax.ppermute(value, axis, [(i, (i + by) % count) for i in range(count)])


def tables(positions, head_width):
    middle = head_width // 2
    frequency = jnp.exp(
        -(2.0 / head_width) * math.log(THETA) * jnp.arange(middle, dtype=jnp.float32)
    )
    angles = positions.astype(jnp.float32)[:, None] * frequency[None, :]
    cosine, sine = jnp.cos(angles), jnp.sin(angles)
    return jnp.concatenate([cosine, cosine], axis=1), jnp.concatenate([-sine, sine], axis=1)

BF16, F32 = jnp.bfloat16, jnp.float32
VMEM_LIMIT = 24 * 1024 * 1024


def call(kernel, outs, scalars, arrays, scratch=(), flops=0):
    whole = pl.BlockSpec(memory_space=pltpu.VMEM)
    specs = [pl.BlockSpec(memory_space=pltpu.SMEM)] * len(scalars)
    specs += [whole] * len(arrays)
    return pl.pallas_call(
        kernel,
        out_shape=[jax.ShapeDtypeStruct(shape, dtype) for shape, dtype in outs],
        in_specs=specs,
        out_specs=[whole] * len(outs),
        scratch_shapes=list(scratch),
        compiler_params=pltpu.CompilerParams(vmem_limit_bytes=VMEM_LIMIT),
        cost_estimate=(
            pl.CostEstimate(flops=flops, bytes_accessed=0, transcendentals=0) if flops else None
        ),
    )(*scalars, *arrays)


def turn(values, cosine, signed_sine):
    return values * cosine + pltpu.roll(values, values.shape[1] // 2, axis=1) * signed_sine


def spread_down(row, size):
    return jnp.transpose(jnp.broadcast_to(row, (size, size)))


def outgoing_kernel(
    sections,
    gain,
    hidden,
    query_weight,
    key_weight,
    value_weight,
    out,
    x,
    keyval_weight,
    tail,
    rows16,
    block_sems,
    weight_sems,
    direct_sems,
    tail_sem,
):
    rows, part = x.shape
    size = BLOCK
    count = rows // size
    width = key_weight.shape[1]
    loads = [
        pltpu.make_async_copy(key_weight, keyval_weight.at[0], weight_sems.at[0]),
        pltpu.make_async_copy(value_weight, keyval_weight.at[1], weight_sems.at[1]),
    ]
    blocks = [
        pltpu.make_async_copy(
            hidden.at[pl.ds(b * size, size), :], x.at[pl.ds(b * size, size), :], block_sems.at[b]
        )
        for b in range(count)
    ]
    direct = [
        pltpu.make_async_copy(
            query_weight.at[pl.ds(t * part, part), :],
            out.at[t, pl.ds(0, part), :],
            direct_sems.at[t],
        )
        for t in range(sections)
    ]
    for copy in loads + blocks + direct:
        copy.start()
    rows16[...] = jnp.zeros_like(rows16)
    for copy in loads:
        copy.wait()
    both_weights = jnp.concatenate([keyval_weight[0], keyval_weight[1]], axis=1)
    for b in range(count):
        blocks[b].wait()
        block = x[b * size : (b + 1) * size, :].astype(F32)
        total = jnp.sum(block * block, axis=1, keepdims=True)
        line = jnp.transpose(jnp.broadcast_to(total, (size, size)))[0:1, :]
        high = line.astype(BF16).astype(F32)
        rows16[b : b + 1, :] = high
        rows16[count + b : count + b + 1, :] = line - high
        block = block * gain[...]
        high = block.astype(BF16)
        low = (block - high.astype(F32)).astype(BF16)
        both = jnp.dot(
            jnp.concatenate([high, low], axis=0), both_weights, preferred_element_type=F32
        )
        both = (both[:size] + both[size:]).astype(BF16)
        tail[b, 0:size, :] = both[:, :width]
        tail[b, size : 2 * size, :] = both[:, width:]
    for t in range(sections):
        tail[t, 2 * size : 2 * size + 16, :] = rows16[...].astype(BF16)
    last = pltpu.make_async_copy(tail, out.at[:, pl.ds(part, 2 * size + 16), :], tail_sem)
    last.start()
    for copy in direct:
        copy.wait()
    last.wait()


def partial_kernel(sections, place, x, gain, arrived, cosine, sine, out, squares, normed):
    rows, part = x.shape
    size = BLOCK
    count = rows // size
    head_width = arrived.shape[2]
    tail = jnp.sum(arrived[:, part + 2 * size : part + 2 * size + 16, :].astype(F32), axis=0)
    squares[0:count, :] = lax.rsqrt(
        (tail[0:count, :] + tail[count : 2 * count, :]) / (part * sections) + EPSILON
    )
    for b in range(count):
        scale = spread_down(squares[b : b + 1, :], size)
        scale = jnp.concatenate([scale] * (part // size), axis=1)
        block = x[b * size : (b + 1) * size, :].astype(F32) * scale * gain[...]
        normed[b * size : (b + 1) * size, :] = block.astype(BF16)
    for k in range(0, sections, 2):
        pair = jnp.concatenate([arrived[k, 0:part, :], arrived[k + 1, 0:part, :]], axis=1)
        value = jnp.dot(normed[...], pair, preferred_element_type=F32).astype(BF16)
        out[k, 0:rows, :] = value[:, :head_width]
        out[k + 1, 0:rows, :] = value[:, head_width:]
    scale = spread_down(squares[pl.ds(place[0], 1), :], size)
    keys = jnp.sum(arrived[:, part : part + size, :].astype(F32), axis=0)
    keys = turn(keys * scale, cosine[...], sine[...]).astype(BF16)
    values = jnp.sum(arrived[:, part + size : part + 2 * size, :].astype(F32), axis=0)
    values = (values * scale).astype(BF16)
    for target in range(sections):
        out[target, rows : rows + size, :] = keys
        out[target, rows + size : rows + 2 * size, :] = values


def finish_kernel(header_ids, arrived, cosine, sine, queries, keyval, picked):
    rows, head_width = queries.shape
    size = BLOCK
    count = rows // size
    for b in range(count):
        part = slice(b * size, (b + 1) * size)
        total = jnp.sum(arrived[:, part, :].astype(F32), axis=0)
        queries[part, :] = turn(total, cosine[part, :], sine[part, :]).astype(BF16)
        keyval[part, 0:head_width] = arrived[b, rows : rows + size, :]
        keyval[part, head_width:] = arrived[b, rows + size : rows + 2 * size, :]
    for h in range(picked.shape[0] // size):
        start = pl.multiple_of(lax.rem(header_ids[h], count) * size, size)
        picked[h * size : (h + 1) * size, 0:head_width] = queries[pl.ds(start, size), :]
        picked[h * size : (h + 1) * size, head_width:] = keyval[pl.ds(start, size), :]


def repeat_kernel(seq_place, header_ids, local_blocks, spread, out):
    header = lax.div(seq_place[0] * spread.shape[1], BLOCK)
    rows = spread[lax.div(header_ids[header], local_blocks[0])]
    out[...] = jnp.broadcast_to(rows[None], out.shape)


def window_kernel(
    total_blocks, seq_place, reach, header_ids, queries, before, here, after, header, out
):
    rows, head_width = queries.shape
    size = BLOCK
    count = rows // size
    parts = [before[j * size : (j + 1) * size, :] for j in range(REACH)]
    parts += [here[j * size : (j + 1) * size, :] for j in range(count)]
    parts += [after[j * size : (j + 1) * size, :] for j in range(REACH)]
    head_keys = header[:, head_width : 2 * head_width]
    head_values = header[:, 2 * head_width :]
    for b in range(count):
        near = parts[b : b + 2 * REACH + 1]
        keys = jnp.concatenate([part[:, :head_width] for part in near] + [head_keys], axis=0)
        values = jnp.concatenate([part[:, head_width:] for part in near] + [head_values], axis=0)
        scores = lax.dot_general(
            queries[b * size : (b + 1) * size, :],
            keys,
            (((1,), (1,)), ((), ())),
            preferred_element_type=F32,
        ) * (1.0 / math.sqrt(head_width))
        pieces = []
        for j in range(2 * REACH + 1):
            block = seq_place[0] * count + b + j - REACH
            allowed = (block >= 0) & (block < total_blocks) & (abs(j - REACH) <= reach[b])
            for h in range(2):
                allowed = allowed & (block != header_ids[h])
            pieces.append(
                jnp.where(allowed, scores[:, j * size : (j + 1) * size], -jnp.inf)
            )
        pieces.append(scores[:, (2 * REACH + 1) * size :])
        scores = jnp.concatenate(pieces, axis=1)
        weights = jnp.exp(scores - jnp.max(scores, axis=1, keepdims=True))
        total = jnp.sum(weights, axis=1, keepdims=True)
        mixed = jnp.dot(weights.astype(BF16), values, preferred_element_type=F32)
        mixed = (mixed / total).astype(BF16)
        out[b * size : (b + 1) * size, :] = jnp.concatenate([mixed, mixed], axis=1)


def far_kernel(header, keyval, out):
    head_width = header.shape[1] // 3
    scores = lax.dot_general(
        header[:, 0:head_width],
        keyval[:, 0:head_width],
        (((1,), (1,)), ((), ())),
        preferred_element_type=F32,
    ) * (1.0 / math.sqrt(head_width))
    top = jnp.max(scores, axis=1, keepdims=True)
    weights = jnp.exp(scores - top)
    total = jnp.sum(weights, axis=1, keepdims=True)
    mixed = jnp.dot(weights.astype(BF16), keyval[:, head_width:], preferred_element_type=F32)
    level = jnp.broadcast_to(top + jnp.log(total), mixed.shape)
    first = level.astype(BF16).astype(F32)
    second = (level - first).astype(BF16).astype(F32)
    lane = lax.broadcasted_iota(jnp.int32, mixed.shape, 1)
    level = jnp.where(lane < 32, first, jnp.where(lane < 64, second, level - first - second))
    out[:, 0:head_width] = (mixed / total).astype(BF16)
    out[:, head_width:] = level.astype(BF16)


def place_kernel(seq_place, header_ids, attended, weight, _, out, block, semaphore):
    size = BLOCK
    count = out.shape[0] // size
    for h in range(2):

        @pl.when(lax.div(header_ids[h], count) == seq_place[0])
        def _():
            rows = slice(h * size, (h + 1) * size)
            left = jnp.concatenate(
                [attended[s, rows, :] for s in range(attended.shape[0])], axis=1
            )
            block[...] = jnp.dot(left, weight[...], preferred_element_type=F32).astype(BF16)
            start = pl.multiple_of(lax.rem(header_ids[h], count) * size, size)
            copy = pltpu.make_async_copy(block, out.at[pl.ds(start, size), :], semaphore)
            copy.start()
            copy.wait()


def merge_kernel(parts, out):
    head_width = out.shape[2]
    everything = parts[...].astype(F32)
    level = everything[:, :, head_width:]
    level = level[:, :, 0:1] + level[:, :, 32:33] + level[:, :, 64:65]
    factor = jnp.exp(level - jnp.max(level, axis=0, keepdims=True))
    total = jnp.sum(everything[:, :, :head_width] * factor, axis=0)
    result = (total / jnp.sum(factor, axis=0)).astype(BF16)
    out[...] = jnp.broadcast_to(result[None], out.shape)


def on_device(
    hidden,
    norm_gain,
    query_weight,
    key_weight,
    value_weight,
    output_weight,
    block_reach,
    header_ids,
):
    bf16, f32 = jnp.bfloat16, jnp.float32
    rows, part = hidden.shape
    head_width = key_weight.shape[1]
    sections = lax.axis_size("section")
    shards = lax.axis_size("seq")
    local_blocks = rows // BLOCK
    total_blocks = local_blocks * shards
    section_place = lax.axis_index("section")
    seq_place = lax.axis_index("seq")
    headers = header_ids.shape[0]
    mine = headers * BLOCK // shards
    gain = norm_gain.astype(f32)[None, :]

    places = [place.astype(jnp.int32).reshape(1) for place in (section_place, seq_place)]
    tall = part + 2 * BLOCK + 16
    hbm = pl.BlockSpec(memory_space=pltpu.HBM)
    outgoing = pl.pallas_call(
        functools.partial(outgoing_kernel, sections),
        out_shape=jax.ShapeDtypeStruct((sections, tall, head_width), bf16),
        in_specs=[pl.BlockSpec(memory_space=pltpu.VMEM)] + [hbm] * 4,
        out_specs=hbm,
        scratch_shapes=[
            pltpu.VMEM((rows, part), bf16),
            pltpu.VMEM((2, part, head_width), bf16),
            pltpu.VMEM((sections, tall - part, head_width), bf16),
            pltpu.VMEM((16, head_width), f32),
            pltpu.SemaphoreType.DMA((local_blocks,)),
            pltpu.SemaphoreType.DMA((2,)),
            pltpu.SemaphoreType.DMA((sections,)),
            pltpu.SemaphoreType.DMA,
        ],
    )(gain, hidden, query_weight, key_weight, value_weight)
    incoming = lax.all_to_all(outgoing, "section", 0, 0)
    own_positions = seq_place * rows + jnp.arange(rows, dtype=jnp.int32)
    own_tables = tables(own_positions, head_width)
    block_tables = [
        lax.dynamic_slice_in_dim(table, section_place * BLOCK, BLOCK, axis=0)
        for table in own_tables
    ]
    (payload,) = call(
        functools.partial(partial_kernel, sections),
        [((sections, rows + 2 * BLOCK, head_width), bf16)],
        [places[0]],
        [hidden, gain, incoming, *block_tables],
        [pltpu.VMEM((8, head_width), f32), pltpu.VMEM((rows, part), bf16)],
    )
    arrived = lax.all_to_all(payload, "section", 0, 0)
    queries, stacked, picked = call(
        finish_kernel,
        [
            ((rows, head_width), bf16),
            ((rows, 2 * head_width), bf16),
            ((headers * BLOCK, 3 * head_width), bf16),
        ],
        [header_ids],
        [arrived, *own_tables],
    )

    spread = lax.all_to_all(picked.reshape(shards, mine, 3 * head_width), "seq", 0, 0)
    (header_copies,) = call(
        repeat_kernel,
        [((shards, mine, 3 * head_width), bf16)],
        [places[1], header_ids, jnp.full((1,), local_blocks, jnp.int32)],
        [spread],
    )
    header_copies, edges = lax.optimization_barrier((header_copies, stacked))
    header_pack = lax.all_to_all(header_copies, "seq", 0, 0).reshape(-1, 3 * head_width)
    margin_rows = REACH * BLOCK
    before = shift(edges[rows - margin_rows :], "seq", 1)
    after = shift(edges[:margin_rows], "seq", -1)
    (partial,) = call(
        far_kernel,
        [((headers * BLOCK, 2 * head_width), bf16)],
        [],
        [header_pack, stacked],
    )
    partial, queries, before, after = lax.optimization_barrier(
        (partial, queries, before, after)
    )
    parts = lax.all_to_all(partial.reshape(shards, mine, 2 * head_width), "seq", 0, 0)
    everywhere = sections * shards
    (mixed,) = call(
        functools.partial(window_kernel, total_blocks),
        [((rows, 2 * head_width), bf16)],
        [places[1], block_reach, header_ids],
        [queries, before, stacked, after, header_pack],
    )
    (result_copies,) = call(
        merge_kernel, [((everywhere, mine, head_width), bf16)], [], [parts], flops=10**11
    )
    result_copies, _ = lax.optimization_barrier((result_copies, mixed))
    header_all = lax.all_to_all(result_copies, ("section", "seq"), 0, 0).reshape(
        sections, headers * BLOCK, head_width
    )
    gathered = lax.all_gather(mixed, "section")
    gathered = jnp.concatenate([gathered[k, :, :head_width] for k in range(sections)], axis=1)
    result = jnp.dot(gathered, output_weight, preferred_element_type=f32).astype(bf16)
    whole = pl.BlockSpec(memory_space=pltpu.VMEM)
    scalar = pl.BlockSpec(memory_space=pltpu.SMEM)
    anywhere = pl.BlockSpec(memory_space=pl.ANY)
    return pl.pallas_call(
        place_kernel,
        out_shape=jax.ShapeDtypeStruct(result.shape, bf16),
        in_specs=[scalar, scalar, whole, whole, anywhere],
        out_specs=anywhere,
        scratch_shapes=[pltpu.VMEM((BLOCK, result.shape[1]), bf16), pltpu.SemaphoreType.DMA],
        input_output_aliases={4: 0},
        compiler_params=pltpu.CompilerParams(vmem_limit_bytes=VMEM_LIMIT),
    )(places[1], header_ids, header_all, output_weight, result)


def solution(mesh):
    return jax.shard_map(
        on_device,
        mesh=mesh,
        in_specs=(
            P("seq", "section"),
            P("section"),
            P(None, "section"),
            P("section", None),
            P("section", None),
            P(None, "section"),
            P("seq"),
            P(),
        ),
        out_specs=P("seq", "section"),
        check_vma=False,
    )
```

```python
import functools
import math

import jax
import jax.numpy as jnp
from jax import lax
from jax.experimental import pallas as pl
from jax.experimental.pallas import tpu as pltpu
from jax.sharding import PartitionSpec as P

BLOCK = 128
REACH = 2

EPSILON = 1e-05
THETA = 500000.0


def shift(value, axis, by):
    count = lax.axis_size(axis)
    return lax.ppermute(value, axis, [(i, (i + by) % count) for i in range(count)])


def tables(positions, head_width):
    middle = head_width // 2
    frequency = jnp.exp(
        -(2.0 / head_width) * math.log(THETA) * jnp.arange(middle, dtype=jnp.float32)
    )
    angles = positions.astype(jnp.float32)[:, None] * frequency[None, :]
    cosine, sine = jnp.cos(angles), jnp.sin(angles)
    return jnp.concatenate([cosine, cosine], axis=1), jnp.concatenate([-sine, sine], axis=1)

BF16, F32 = jnp.bfloat16, jnp.float32
VMEM_LIMIT = 24 * 1024 * 1024


def call(kernel, outs, scalars, arrays, scratch=(), flops=0):
    whole = pl.BlockSpec(memory_space=pltpu.VMEM)
    specs = [pl.BlockSpec(memory_space=pltpu.SMEM)] * len(scalars)
    specs += [whole] * len(arrays)
    return pl.pallas_call(
        kernel,
        out_shape=[jax.ShapeDtypeStruct(shape, dtype) for shape, dtype in outs],
        in_specs=specs,
        out_specs=[whole] * len(outs),
        scratch_shapes=list(scratch),
        compiler_params=pltpu.CompilerParams(vmem_limit_bytes=VMEM_LIMIT),
        cost_estimate=(
            pl.CostEstimate(flops=flops, bytes_accessed=0, transcendentals=0) if flops else None
        ),
    )(*scalars, *arrays)


def turn(values, cosine, signed_sine):
    return values * cosine + pltpu.roll(values, values.shape[1] // 2, axis=1) * signed_sine


def spread_down(row, size):
    return jnp.transpose(jnp.broadcast_to(row, (size, size)))


def outgoing_kernel(
    sections,
    gain,
    hidden,
    query_weight,
    key_weight,
    value_weight,
    out,
    x,
    keyval_weight,
    stage,
    tail,
    rows16,
    block_sems,
    weight_sems,
    stage_sems,
    direct_sems,
    tail_sem,
):
    rows, part = x.shape
    size = BLOCK
    count = rows // size
    width = key_weight.shape[1]
    loads = [
        pltpu.make_async_copy(key_weight, keyval_weight.at[0], weight_sems.at[0]),
        pltpu.make_async_copy(value_weight, keyval_weight.at[1], weight_sems.at[1]),
    ]
    blocks = [
        pltpu.make_async_copy(
            hidden.at[pl.ds(b * size, size), :], x.at[pl.ds(b * size, size), :], block_sems.at[b]
        )
        for b in range(count)
    ]
    staged = [
        pltpu.make_async_copy(
            query_weight.at[pl.ds(t * part, part), :], stage.at[t], stage_sems.at[t]
        )
        for t in range(sections)
    ]
    direct = [
        pltpu.make_async_copy(stage.at[t], out.at[t, pl.ds(0, part), :], direct_sems.at[t])
        for t in range(sections)
    ]
    for copy in loads + blocks + staged:
        copy.start()
    rows16[...] = jnp.zeros_like(rows16)
    factor = gain[...].astype(F32).reshape(1, part)
    for copy in loads:
        copy.wait()
    both_weights = jnp.concatenate([keyval_weight[0], keyval_weight[1]], axis=1)
    for b in range(count):
        blocks[b].wait()
        staged[b].wait()
        direct[b].start()
        block = x[b * size : (b + 1) * size, :].astype(F32)
        total = jnp.sum(block * block, axis=1, keepdims=True)
        line = jnp.transpose(jnp.broadcast_to(total, (size, size)))[0:1, :]
        high = line.astype(BF16).astype(F32)
        rows16[b : b + 1, :] = high
        rows16[count + b : count + b + 1, :] = line - high
        block = block * factor
        high = block.astype(BF16)
        low = (block - high.astype(F32)).astype(BF16)
        both = jnp.dot(
            jnp.concatenate([high, low], axis=0), both_weights, preferred_element_type=F32
        )
        both = (both[:size] + both[size:]).astype(BF16)
        tail[b, 0:size, :] = both[:, :width]
        tail[b, size : 2 * size, :] = both[:, width:]
    for t in range(sections):
        tail[t, 2 * size : 2 * size + 16, :] = rows16[...].astype(BF16)
    last = pltpu.make_async_copy(tail, out.at[:, pl.ds(part, 2 * size + 16), :], tail_sem)
    last.start()
    for copy in direct + [last]:
        copy.wait()


def partial_kernel(sections, place, x, gain, arrived, cosine, sine, out, squares, normed):
    rows, part = x.shape
    size = BLOCK
    count = rows // size
    head_width = arrived.shape[2]
    tail = jnp.sum(arrived[:, part + 2 * size : part + 2 * size + 16, :].astype(F32), axis=0)
    squares[0:count, :] = lax.rsqrt(
        (tail[0:count, :] + tail[count : 2 * count, :]) / (part * sections) + EPSILON
    )
    for b in range(count):
        scale = spread_down(squares[b : b + 1, :], size)
        scale = jnp.concatenate([scale] * (part // size), axis=1)
        block = x[b * size : (b + 1) * size, :].astype(F32) * scale * gain[...].astype(F32)
        normed[b * size : (b + 1) * size, :] = block.astype(BF16)
    for k in range(0, sections, 2):
        pair = jnp.concatenate([arrived[k, 0:part, :], arrived[k + 1, 0:part, :]], axis=1)
        value = jnp.dot(normed[...], pair, preferred_element_type=F32).astype(BF16)
        out[k, 0:rows, :] = value[:, :head_width]
        out[k + 1, 0:rows, :] = value[:, head_width:]
    scale = spread_down(squares[pl.ds(place[0], 1), :], size)
    keys = jnp.sum(arrived[:, part : part + size, :].astype(F32), axis=0)
    keys = turn(keys * scale, cosine[...], sine[...]).astype(BF16)
    values = jnp.sum(arrived[:, part + size : part + 2 * size, :].astype(F32), axis=0)
    values = (values * scale).astype(BF16)
    for target in range(sections):
        out[target, rows : rows + size, :] = keys
        out[target, rows + size : rows + 2 * size, :] = values


def finish_kernel(header_ids, arrived, cosine, sine, queries, keyval, picked):
    rows, head_width = queries.shape
    size = BLOCK
    count = rows // size
    for b in range(count):
        part = slice(b * size, (b + 1) * size)
        total = jnp.sum(arrived[:, part, :].astype(F32), axis=0)
        queries[part, :] = turn(total, cosine[part, :], sine[part, :]).astype(BF16)
        keyval[part, 0:head_width] = arrived[b, rows : rows + size, :]
        keyval[part, head_width:] = arrived[b, rows + size : rows + 2 * size, :]
    for h in range(picked.shape[0] // size):
        start = pl.multiple_of(lax.rem(header_ids[h], count) * size, size)
        picked[h * size : (h + 1) * size, 0:head_width] = queries[pl.ds(start, size), :]
        picked[h * size : (h + 1) * size, head_width:] = keyval[pl.ds(start, size), :]


def repeat_kernel(seq_place, header_ids, local_blocks, spread, out):
    header = lax.div(seq_place[0] * spread.shape[1], BLOCK)
    rows = spread[lax.div(header_ids[header], local_blocks[0])]
    out[...] = jnp.broadcast_to(rows[None], out.shape)


def window_kernel(
    total_blocks, seq_place, reach, header_ids, queries, before, here, after, header, out
):
    rows, head_width = queries.shape
    size = BLOCK
    count = rows // size
    parts = [before[j * size : (j + 1) * size, :] for j in range(REACH)]
    parts += [here[j * size : (j + 1) * size, :] for j in range(count)]
    parts += [after[j * size : (j + 1) * size, :] for j in range(REACH)]
    head_keys = header[:, head_width : 2 * head_width]
    head_values = header[:, 2 * head_width :]
    for b in range(count):
        near = parts[b : b + 2 * REACH + 1]
        keys = jnp.concatenate([part[:, :head_width] for part in near] + [head_keys], axis=0)
        values = jnp.concatenate([part[:, head_width:] for part in near] + [head_values], axis=0)
        scores = lax.dot_general(
            queries[b * size : (b + 1) * size, :],
            keys,
            (((1,), (1,)), ((), ())),
            preferred_element_type=F32,
        ) * (1.0 / math.sqrt(head_width))
        pieces = []
        for j in range(2 * REACH + 1):
            block = seq_place[0] * count + b + j - REACH
            allowed = (block >= 0) & (block < total_blocks) & (abs(j - REACH) <= reach[b])
            for h in range(2):
                allowed = allowed & (block != header_ids[h])
            pieces.append(
                jnp.where(allowed, scores[:, j * size : (j + 1) * size], -jnp.inf)
            )
        pieces.append(scores[:, (2 * REACH + 1) * size :])
        scores = jnp.concatenate(pieces, axis=1)
        weights = jnp.exp(scores - jnp.max(scores, axis=1, keepdims=True))
        total = jnp.sum(weights, axis=1, keepdims=True)
        mixed = jnp.dot(weights.astype(BF16), values, preferred_element_type=F32)
        mixed = (mixed / total).astype(BF16)
        out[b * size : (b + 1) * size, :] = jnp.concatenate([mixed, mixed], axis=1)


def far_kernel(header, keyval, out):
    head_width = header.shape[1] // 3
    scores = lax.dot_general(
        header[:, 0:head_width],
        keyval[:, 0:head_width],
        (((1,), (1,)), ((), ())),
        preferred_element_type=F32,
    ) * (1.0 / math.sqrt(head_width))
    top = jnp.max(scores, axis=1, keepdims=True)
    weights = jnp.exp(scores - top)
    total = jnp.sum(weights, axis=1, keepdims=True)
    mixed = jnp.dot(weights.astype(BF16), keyval[:, head_width:], preferred_element_type=F32)
    level = jnp.broadcast_to(top + jnp.log(total), mixed.shape)
    first = level.astype(BF16).astype(F32)
    second = (level - first).astype(BF16).astype(F32)
    lane = lax.broadcasted_iota(jnp.int32, mixed.shape, 1)
    level = jnp.where(lane < 32, first, jnp.where(lane < 64, second, level - first - second))
    out[:, 0:head_width] = (mixed / total).astype(BF16)
    out[:, head_width:] = level.astype(BF16)


def place_kernel(seq_place, header_ids, attended, weight, _, out, block, semaphore):
    size = BLOCK
    count = out.shape[0] // size
    for h in range(2):

        @pl.when(lax.div(header_ids[h], count) == seq_place[0])
        def _():
            rows = slice(h * size, (h + 1) * size)
            left = jnp.concatenate(
                [attended[s, rows, :] for s in range(attended.shape[0])], axis=1
            )
            block[...] = jnp.dot(left, weight[...], preferred_element_type=F32).astype(BF16)
            start = pl.multiple_of(lax.rem(header_ids[h], count) * size, size)
            copy = pltpu.make_async_copy(block, out.at[pl.ds(start, size), :], semaphore)
            copy.start()
            copy.wait()


def merge_kernel(parts, out):
    head_width = out.shape[2]
    everything = parts[...].astype(F32)
    level = everything[:, :, head_width:]
    level = level[:, :, 0:1] + level[:, :, 32:33] + level[:, :, 64:65]
    factor = jnp.exp(level - jnp.max(level, axis=0, keepdims=True))
    total = jnp.sum(everything[:, :, :head_width] * factor, axis=0)
    result = (total / jnp.sum(factor, axis=0)).astype(BF16)
    out[...] = jnp.broadcast_to(result[None], out.shape)


def on_device(
    hidden,
    norm_gain,
    query_weight,
    key_weight,
    value_weight,
    output_weight,
    block_reach,
    header_ids,
):
    bf16, f32 = jnp.bfloat16, jnp.float32
    rows, part = hidden.shape
    head_width = key_weight.shape[1]
    sections = lax.axis_size("section")
    shards = lax.axis_size("seq")
    local_blocks = rows // BLOCK
    total_blocks = local_blocks * shards
    section_place = lax.axis_index("section")
    seq_place = lax.axis_index("seq")
    headers = header_ids.shape[0]
    mine = headers * BLOCK // shards
    gain = norm_gain[None, :]

    places = [place.astype(jnp.int32).reshape(1) for place in (section_place, seq_place)]
    tall = part + 2 * BLOCK + 16
    hbm = pl.BlockSpec(memory_space=pltpu.HBM)
    outgoing = pl.pallas_call(
        functools.partial(outgoing_kernel, sections),
        out_shape=jax.ShapeDtypeStruct((sections, tall, head_width), bf16),
        in_specs=[pl.BlockSpec(memory_space=pltpu.VMEM)] + [hbm] * 4,
        out_specs=hbm,
        scratch_shapes=[
            pltpu.VMEM((rows, part), bf16),
            pltpu.VMEM((2, part, head_width), bf16),
            pltpu.VMEM((sections, part, head_width), bf16),
            pltpu.VMEM((sections, 2 * BLOCK + 16, head_width), bf16),
            pltpu.VMEM((16, head_width), f32),
            pltpu.SemaphoreType.DMA((local_blocks,)),
            pltpu.SemaphoreType.DMA((2,)),
            pltpu.SemaphoreType.DMA((sections,)),
            pltpu.SemaphoreType.DMA((sections,)),
            pltpu.SemaphoreType.DMA,
        ],
    )(norm_gain, hidden, query_weight, key_weight, value_weight)
    incoming = lax.all_to_all(outgoing, "section", 0, 0)
    own_positions = seq_place * rows + jnp.arange(rows, dtype=jnp.int32)
    own_tables = tables(own_positions, head_width)
    block_tables = [
        lax.dynamic_slice_in_dim(table, section_place * BLOCK, BLOCK, axis=0)
        for table in own_tables
    ]
    (payload,) = call(
        functools.partial(partial_kernel, sections),
        [((sections, rows + 2 * BLOCK, head_width), bf16)],
        [places[0]],
        [hidden, gain, incoming, *block_tables],
        [pltpu.VMEM((8, head_width), f32), pltpu.VMEM((rows, part), bf16)],
    )
    arrived = lax.all_to_all(payload, "section", 0, 0)
    queries, stacked, picked = call(
        finish_kernel,
        [
            ((rows, head_width), bf16),
            ((rows, 2 * head_width), bf16),
            ((headers * BLOCK, 3 * head_width), bf16),
        ],
        [header_ids],
        [arrived, *own_tables],
    )

    spread = lax.all_to_all(picked.reshape(shards, mine, 3 * head_width), "seq", 0, 0)
    (header_copies,) = call(
        repeat_kernel,
        [((shards, mine, 3 * head_width), bf16)],
        [places[1], header_ids, jnp.full((1,), local_blocks, jnp.int32)],
        [spread],
    )
    header_copies, edges = lax.optimization_barrier((header_copies, stacked))
    header_pack = lax.all_to_all(header_copies, "seq", 0, 0).reshape(-1, 3 * head_width)
    margin_rows = REACH * BLOCK
    before = shift(edges[rows - margin_rows :], "seq", 1)
    after = shift(edges[:margin_rows], "seq", -1)
    (partial,) = call(
        far_kernel,
        [((headers * BLOCK, 2 * head_width), bf16)],
        [],
        [header_pack, stacked],
    )
    partial, queries, before, after = lax.optimization_barrier(
        (partial, queries, before, after)
    )
    parts = lax.all_to_all(partial.reshape(shards, mine, 2 * head_width), "seq", 0, 0)
    everywhere = sections * shards
    (mixed,) = call(
        functools.partial(window_kernel, total_blocks),
        [((rows, 2 * head_width), bf16)],
        [places[1], block_reach, header_ids],
        [queries, before, stacked, after, header_pack],
    )
    (result_copies,) = call(
        merge_kernel, [((everywhere, mine, head_width), bf16)], [], [parts], flops=10**11
    )
    result_copies, _ = lax.optimization_barrier((result_copies, mixed))
    header_all = lax.all_to_all(result_copies, ("section", "seq"), 0, 0).reshape(
        sections, headers * BLOCK, head_width
    )
    gathered = lax.all_gather(mixed, "section")
    gathered = jnp.concatenate([gathered[k, :, :head_width] for k in range(sections)], axis=1)
    result = jnp.dot(gathered, output_weight, preferred_element_type=f32).astype(bf16)
    whole = pl.BlockSpec(memory_space=pltpu.VMEM)
    scalar = pl.BlockSpec(memory_space=pltpu.SMEM)
    anywhere = pl.BlockSpec(memory_space=pl.ANY)
    return pl.pallas_call(
        place_kernel,
        out_shape=jax.ShapeDtypeStruct(result.shape, bf16),
        in_specs=[scalar, scalar, whole, whole, anywhere],
        out_specs=anywhere,
        scratch_shapes=[pltpu.VMEM((BLOCK, result.shape[1]), bf16), pltpu.SemaphoreType.DMA],
        input_output_aliases={4: 0},
        compiler_params=pltpu.CompilerParams(vmem_limit_bytes=VMEM_LIMIT),
    )(places[1], header_ids, header_all, output_weight, result)


def solution(mesh):
    return jax.shard_map(
        on_device,
        mesh=mesh,
        in_specs=(
            P("seq", "section"),
            P("section"),
            P(None, "section"),
            P("section", None),
            P("section", None),
            P(None, "section"),
            P("seq"),
            P(),
        ),
        out_specs=P("seq", "section"),
        check_vma=False,
    )
```

```python
import functools
import math

import jax
import jax.numpy as jnp
from jax import lax
from jax.experimental import pallas as pl
from jax.experimental.pallas import tpu as pltpu
from jax.sharding import PartitionSpec as P

BLOCK = 128
REACH = 2

EPSILON = 1e-05
THETA = 500000.0


def shift(value, axis, by):
    count = lax.axis_size(axis)
    return lax.ppermute(value, axis, [(i, (i + by) % count) for i in range(count)])


def tables(positions, head_width):
    middle = head_width // 2
    frequency = jnp.exp(
        -(2.0 / head_width) * math.log(THETA) * jnp.arange(middle, dtype=jnp.float32)
    )
    angles = positions.astype(jnp.float32)[:, None] * frequency[None, :]
    cosine, sine = jnp.cos(angles), jnp.sin(angles)
    return jnp.concatenate([cosine, cosine], axis=1), jnp.concatenate([-sine, sine], axis=1)

BF16, F32 = jnp.bfloat16, jnp.float32
VMEM_LIMIT = 24 * 1024 * 1024


def call(kernel, outs, scalars, arrays, scratch=()):
    whole = pl.BlockSpec(memory_space=pltpu.VMEM)
    specs = [pl.BlockSpec(memory_space=pltpu.SMEM)] * len(scalars)
    specs += [whole] * len(arrays)
    return pl.pallas_call(
        kernel,
        out_shape=[jax.ShapeDtypeStruct(shape, dtype) for shape, dtype in outs],
        in_specs=specs,
        out_specs=[whole] * len(outs),
        scratch_shapes=list(scratch),
        compiler_params=pltpu.CompilerParams(vmem_limit_bytes=VMEM_LIMIT),
    )(*scalars, *arrays)


def turn(values, cosine, signed_sine):
    return values * cosine + pltpu.roll(values, values.shape[1] // 2, axis=1) * signed_sine


def spread_down(row, size):
    return jnp.transpose(jnp.broadcast_to(row, (size, size)))


def outgoing_kernel(
    sections,
    gain,
    hidden,
    query_weight,
    key_weight,
    value_weight,
    out,
    x,
    keyval_weight,
    stage,
    tail,
    rows16,
    block_sems,
    weight_sems,
    stage_sems,
    direct_sems,
    tail_sem,
):
    rows, part = x.shape
    size = BLOCK
    count = rows // size
    width = key_weight.shape[1]
    loads = [
        pltpu.make_async_copy(key_weight, keyval_weight.at[0], weight_sems.at[0]),
        pltpu.make_async_copy(value_weight, keyval_weight.at[1], weight_sems.at[1]),
    ]
    blocks = [
        pltpu.make_async_copy(
            hidden.at[pl.ds(b * size, size), :], x.at[pl.ds(b * size, size), :], block_sems.at[b]
        )
        for b in range(count)
    ]
    staged = [
        pltpu.make_async_copy(
            query_weight.at[pl.ds(t * part, part), :], stage.at[t], stage_sems.at[t]
        )
        for t in range(sections)
    ]
    direct = [
        pltpu.make_async_copy(stage.at[t], out.at[t, pl.ds(0, part), :], direct_sems.at[t])
        for t in range(sections)
    ]
    for copy in loads + blocks + staged:
        copy.start()
    rows16[...] = jnp.zeros_like(rows16)
    factor = gain[...].astype(F32).reshape(1, part)
    for copy in loads:
        copy.wait()
    both_weights = jnp.concatenate([keyval_weight[0], keyval_weight[1]], axis=1)
    for b in range(count):
        blocks[b].wait()
        staged[b].wait()
        direct[b].start()
        block = x[b * size : (b + 1) * size, :].astype(F32)
        total = jnp.sum(block * block, axis=1, keepdims=True)
        line = jnp.transpose(jnp.broadcast_to(total, (size, size)))[0:1, :]
        high = line.astype(BF16).astype(F32)
        rows16[b : b + 1, :] = high
        rows16[count + b : count + b + 1, :] = line - high
        block = block * factor
        high = block.astype(BF16)
        low = (block - high.astype(F32)).astype(BF16)
        both = jnp.dot(
            jnp.concatenate([high, low], axis=0), both_weights, preferred_element_type=F32
        )
        both = (both[:size] + both[size:]).astype(BF16)
        tail[b, 0:size, :] = both[:, :width]
        tail[b, size : 2 * size, :] = both[:, width:]
    for t in range(sections):
        tail[t, 2 * size : 2 * size + 16, :] = rows16[...].astype(BF16)
    last = pltpu.make_async_copy(tail, out.at[:, pl.ds(part, 2 * size + 16), :], tail_sem)
    last.start()
    for copy in direct + [last]:
        copy.wait()


def partial_kernel(sections, place, x, gain, arrived, cosine, sine, out, squares, normed):
    rows, part = x.shape
    size = BLOCK
    count = rows // size
    head_width = arrived.shape[2]
    tail = jnp.sum(arrived[:, part + 2 * size : part + 2 * size + 16, :].astype(F32), axis=0)
    squares[0:count, :] = lax.rsqrt(
        (tail[0:count, :] + tail[count : 2 * count, :]) / (part * sections) + EPSILON
    )
    for b in range(count):
        scale = spread_down(squares[b : b + 1, :], size)
        scale = jnp.concatenate([scale] * (part // size), axis=1)
        block = x[b * size : (b + 1) * size, :].astype(F32) * scale * gain[...].astype(F32)
        normed[b * size : (b + 1) * size, :] = block.astype(BF16)
    for k in range(0, sections, 2):
        pair = jnp.concatenate([arrived[k, 0:part, :], arrived[k + 1, 0:part, :]], axis=1)
        value = jnp.dot(normed[...], pair, preferred_element_type=F32).astype(BF16)
        out[k, 0:rows, :] = value[:, :head_width]
        out[k + 1, 0:rows, :] = value[:, head_width:]
    scale = spread_down(squares[pl.ds(place[0], 1), :], size)
    keys = jnp.sum(arrived[:, part : part + size, :].astype(F32), axis=0)
    keys = turn(keys * scale, cosine[...], sine[...]).astype(BF16)
    values = jnp.sum(arrived[:, part + size : part + 2 * size, :].astype(F32), axis=0)
    values = (values * scale).astype(BF16)
    for target in range(sections):
        out[target, rows : rows + size, :] = keys
        out[target, rows + size : rows + 2 * size, :] = values


def finish_kernel(header_ids, arrived, cosine, sine, queries, keyval, picked):
    rows, head_width = queries.shape
    size = BLOCK
    count = rows // size
    for b in range(count):
        part = slice(b * size, (b + 1) * size)
        total = jnp.sum(arrived[:, part, :].astype(F32), axis=0)
        queries[part, :] = turn(total, cosine[part, :], sine[part, :]).astype(BF16)
        keyval[part, 0:head_width] = arrived[b, rows : rows + size, :]
        keyval[part, head_width:] = arrived[b, rows + size : rows + 2 * size, :]
    for h in range(picked.shape[0] // size):
        start = pl.multiple_of(lax.rem(header_ids[h], count) * size, size)
        picked[h * size : (h + 1) * size, 0:head_width] = queries[pl.ds(start, size), :]
        picked[h * size : (h + 1) * size, head_width:] = keyval[pl.ds(start, size), :]


def repeat_kernel(seq_place, header_ids, local_blocks, spread, out):
    header = lax.div(seq_place[0] * spread.shape[1], BLOCK)
    rows = spread[lax.div(header_ids[header], local_blocks[0])]
    out[...] = jnp.broadcast_to(rows[None], out.shape)


def window_kernel(
    total_blocks, seq_place, reach, header_ids, queries, before, here, after, header, out
):
    rows, head_width = queries.shape
    size = BLOCK
    count = rows // size
    parts = [before[j * size : (j + 1) * size, :] for j in range(REACH)]
    parts += [here[j * size : (j + 1) * size, :] for j in range(count)]
    parts += [after[j * size : (j + 1) * size, :] for j in range(REACH)]
    head_keys = header[:, head_width : 2 * head_width]
    head_values = header[:, 2 * head_width :]
    for b in range(count):
        near = parts[b : b + 2 * REACH + 1]
        keys = jnp.concatenate([part[:, :head_width] for part in near] + [head_keys], axis=0)
        values = jnp.concatenate([part[:, head_width:] for part in near] + [head_values], axis=0)
        scores = lax.dot_general(
            queries[b * size : (b + 1) * size, :],
            keys,
            (((1,), (1,)), ((), ())),
            preferred_element_type=F32,
        ) * (1.0 / math.sqrt(head_width))
        pieces = []
        for j in range(2 * REACH + 1):
            block = seq_place[0] * count + b + j - REACH
            allowed = (block >= 0) & (block < total_blocks) & (abs(j - REACH) <= reach[b])
            for h in range(2):
                allowed = allowed & (block != header_ids[h])
            pieces.append(
                jnp.where(allowed, scores[:, j * size : (j + 1) * size], -jnp.inf)
            )
        pieces.append(scores[:, (2 * REACH + 1) * size :])
        scores = jnp.concatenate(pieces, axis=1)
        weights = jnp.exp(scores - jnp.max(scores, axis=1, keepdims=True))
        total = jnp.sum(weights, axis=1, keepdims=True)
        mixed = jnp.dot(weights.astype(BF16), values, preferred_element_type=F32)
        out[b * size : (b + 1) * size, :] = (mixed / total).astype(BF16)


def far_kernel(header, keyval, out):
    head_width = header.shape[1] // 3
    scores = lax.dot_general(
        header[:, 0:head_width],
        keyval[:, 0:head_width],
        (((1,), (1,)), ((), ())),
        preferred_element_type=F32,
    ) * (1.0 / math.sqrt(head_width))
    top = jnp.max(scores, axis=1, keepdims=True)
    weights = jnp.exp(scores - top)
    total = jnp.sum(weights, axis=1, keepdims=True)
    mixed = jnp.dot(weights.astype(BF16), keyval[:, head_width:], preferred_element_type=F32)
    level = jnp.broadcast_to(top + jnp.log(total), mixed.shape)
    first = level.astype(BF16).astype(F32)
    second = (level - first).astype(BF16).astype(F32)
    lane = lax.broadcasted_iota(jnp.int32, mixed.shape, 1)
    level = jnp.where(lane < 32, first, jnp.where(lane < 64, second, level - first - second))
    out[:, 0:head_width] = (mixed / total).astype(BF16)
    out[:, head_width:] = level.astype(BF16)


def place_kernel(seq_place, header_ids, attended, weight, _, out, block, semaphore):
    size = BLOCK
    count = out.shape[0] // size
    for h in range(2):

        @pl.when(lax.div(header_ids[h], count) == seq_place[0])
        def _():
            rows = slice(h * size, (h + 1) * size)
            left = jnp.concatenate(
                [attended[s, rows, :] for s in range(attended.shape[0])], axis=1
            )
            block[...] = jnp.dot(left, weight[...], preferred_element_type=F32).astype(BF16)
            start = pl.multiple_of(lax.rem(header_ids[h], count) * size, size)
            copy = pltpu.make_async_copy(block, out.at[pl.ds(start, size), :], semaphore)
            copy.start()
            copy.wait()


def merge_kernel(parts, out):
    head_width = out.shape[2]
    everything = parts[...].astype(F32)
    level = everything[:, :, head_width:]
    level = level[:, :, 0:1] + level[:, :, 32:33] + level[:, :, 64:65]
    factor = jnp.exp(level - jnp.max(level, axis=0, keepdims=True))
    total = jnp.sum(everything[:, :, :head_width] * factor, axis=0)
    result = (total / jnp.sum(factor, axis=0)).astype(BF16)
    out[...] = jnp.broadcast_to(result[None], out.shape)


def on_device(
    hidden,
    norm_gain,
    query_weight,
    key_weight,
    value_weight,
    output_weight,
    block_reach,
    header_ids,
):
    bf16, f32 = jnp.bfloat16, jnp.float32
    rows, part = hidden.shape
    head_width = key_weight.shape[1]
    sections = lax.axis_size("section")
    shards = lax.axis_size("seq")
    local_blocks = rows // BLOCK
    total_blocks = local_blocks * shards
    section_place = lax.axis_index("section")
    seq_place = lax.axis_index("seq")
    headers = header_ids.shape[0]
    mine = headers * BLOCK // shards
    gain = norm_gain[None, :]

    places = [place.astype(jnp.int32).reshape(1) for place in (section_place, seq_place)]
    tall = part + 2 * BLOCK + 16
    hbm = pl.BlockSpec(memory_space=pltpu.HBM)
    outgoing = pl.pallas_call(
        functools.partial(outgoing_kernel, sections),
        out_shape=jax.ShapeDtypeStruct((sections, tall, head_width), bf16),
        in_specs=[pl.BlockSpec(memory_space=pltpu.VMEM)] + [hbm] * 4,
        out_specs=hbm,
        scratch_shapes=[
            pltpu.VMEM((rows, part), bf16),
            pltpu.VMEM((2, part, head_width), bf16),
            pltpu.VMEM((sections, part, head_width), bf16),
            pltpu.VMEM((sections, 2 * BLOCK + 16, head_width), bf16),
            pltpu.VMEM((16, head_width), f32),
            pltpu.SemaphoreType.DMA((local_blocks,)),
            pltpu.SemaphoreType.DMA((2,)),
            pltpu.SemaphoreType.DMA((sections,)),
            pltpu.SemaphoreType.DMA((sections,)),
            pltpu.SemaphoreType.DMA,
        ],
    )(norm_gain, hidden, query_weight, key_weight, value_weight)
    incoming = lax.all_to_all(outgoing, "section", 0, 0)
    own_positions = seq_place * rows + jnp.arange(rows, dtype=jnp.int32)
    own_tables = tables(own_positions, head_width)
    block_tables = [
        lax.dynamic_slice_in_dim(table, section_place * BLOCK, BLOCK, axis=0)
        for table in own_tables
    ]
    (payload,) = call(
        functools.partial(partial_kernel, sections),
        [((sections, rows + 2 * BLOCK, head_width), bf16)],
        [places[0]],
        [hidden, gain, incoming, *block_tables],
        [pltpu.VMEM((8, head_width), f32), pltpu.VMEM((rows, part), bf16)],
    )
    arrived = lax.all_to_all(payload, "section", 0, 0)
    queries, stacked, picked = call(
        finish_kernel,
        [
            ((rows, head_width), bf16),
            ((rows, 2 * head_width), bf16),
            ((headers * BLOCK, 3 * head_width), bf16),
        ],
        [header_ids],
        [arrived, *own_tables],
    )

    spread = lax.all_to_all(picked.reshape(shards, mine, 3 * head_width), "seq", 0, 0)
    (header_copies,) = call(
        repeat_kernel,
        [((shards, mine, 3 * head_width), bf16)],
        [places[1], header_ids, jnp.full((1,), local_blocks, jnp.int32)],
        [spread],
    )
    header_copies, edges = lax.optimization_barrier((header_copies, stacked))
    header_pack = lax.all_to_all(header_copies, "seq", 0, 0).reshape(-1, 3 * head_width)
    margin_rows = REACH * BLOCK
    before = shift(edges[rows - margin_rows :], "seq", 1)
    after = shift(edges[:margin_rows], "seq", -1)
    (partial,) = call(
        far_kernel,
        [((headers * BLOCK, 2 * head_width), bf16)],
        [],
        [header_pack, stacked],
    )
    partial, queries, before, after = lax.optimization_barrier(
        (partial, queries, before, after)
    )
    parts = lax.all_to_all(partial.reshape(shards, mine, 2 * head_width), "seq", 0, 0)
    everywhere = sections * shards
    (mixed,) = call(
        functools.partial(window_kernel, total_blocks),
        [((rows, head_width), bf16)],
        [places[1], block_reach, header_ids],
        [queries, before, stacked, after, header_pack],
    )
    (result_copies,) = call(
        merge_kernel, [((everywhere, mine, head_width), bf16)], [], [parts]
    )
    result_copies, mixed = lax.optimization_barrier((result_copies, mixed))
    header_all = lax.all_to_all(result_copies, ("section", "seq"), 0, 0).reshape(
        sections, headers * BLOCK, head_width
    )
    gathered = lax.all_gather(mixed, "section", axis=1, tiled=True)
    result = jnp.dot(gathered, output_weight, preferred_element_type=f32).astype(bf16)
    whole = pl.BlockSpec(memory_space=pltpu.VMEM)
    scalar = pl.BlockSpec(memory_space=pltpu.SMEM)
    anywhere = pl.BlockSpec(memory_space=pl.ANY)
    return pl.pallas_call(
        place_kernel,
        out_shape=jax.ShapeDtypeStruct(result.shape, bf16),
        in_specs=[scalar, scalar, whole, whole, anywhere],
        out_specs=anywhere,
        scratch_shapes=[pltpu.VMEM((BLOCK, result.shape[1]), bf16), pltpu.SemaphoreType.DMA],
        input_output_aliases={4: 0},
        compiler_params=pltpu.CompilerParams(vmem_limit_bytes=VMEM_LIMIT),
    )(places[1], header_ids, header_all, output_weight, result)


def solution(mesh):
    return jax.shard_map(
        on_device,
        mesh=mesh,
        in_specs=(
            P("seq", "section"),
            P("section"),
            P(None, "section"),
            P("section", None),
            P("section", None),
            P(None, "section"),
            P("seq"),
            P(),
        ),
        out_specs=P("seq", "section"),
        check_vma=False,
    )
```

```python
import functools
import math

import jax
import jax.numpy as jnp
from jax import lax
from jax.experimental import pallas as pl
from jax.experimental.pallas import tpu as pltpu
from jax.sharding import PartitionSpec as P

BLOCK = 128
REACH = 2

EPSILON = 1e-05
THETA = 500000.0


def shift(value, axis, by):
    count = lax.axis_size(axis)
    return lax.ppermute(value, axis, [(i, (i + by) % count) for i in range(count)])


def tables(positions, head_width):
    middle = head_width // 2
    frequency = jnp.exp(
        -(2.0 / head_width) * math.log(THETA) * jnp.arange(middle, dtype=jnp.float32)
    )
    angles = positions.astype(jnp.float32)[:, None] * frequency[None, :]
    cosine, sine = jnp.cos(angles), jnp.sin(angles)
    return jnp.concatenate([cosine, cosine], axis=1), jnp.concatenate([-sine, sine], axis=1)

BF16, F32 = jnp.bfloat16, jnp.float32
VMEM_LIMIT = 24 * 1024 * 1024


def call(kernel, outs, scalars, arrays, scratch=()):
    whole = pl.BlockSpec(memory_space=pltpu.VMEM)
    specs = [pl.BlockSpec(memory_space=pltpu.SMEM)] * len(scalars)
    specs += [whole] * len(arrays)
    return pl.pallas_call(
        kernel,
        out_shape=[jax.ShapeDtypeStruct(shape, dtype) for shape, dtype in outs],
        in_specs=specs,
        out_specs=[whole] * len(outs),
        scratch_shapes=list(scratch),
        compiler_params=pltpu.CompilerParams(vmem_limit_bytes=VMEM_LIMIT),
    )(*scalars, *arrays)


def turn(values, cosine, signed_sine):
    return values * cosine + pltpu.roll(values, values.shape[1] // 2, axis=1) * signed_sine


def spread_down(row, size):
    return jnp.transpose(jnp.broadcast_to(row, (size, size)))


def outgoing_kernel(
    sections,
    gain,
    hidden,
    query_weight,
    key_weight,
    value_weight,
    out,
    x,
    keyval_weight,
    stage,
    tail,
    rows16,
    block_sems,
    weight_sems,
    stage_sems,
    direct_sems,
    tail_sem,
):
    rows, part = x.shape
    size = BLOCK
    count = rows // size
    width = key_weight.shape[1]
    loads = [
        pltpu.make_async_copy(key_weight, keyval_weight.at[0], weight_sems.at[0]),
        pltpu.make_async_copy(value_weight, keyval_weight.at[1], weight_sems.at[1]),
    ]
    blocks = [
        pltpu.make_async_copy(
            hidden.at[pl.ds(b * size, size), :], x.at[pl.ds(b * size, size), :], block_sems.at[b]
        )
        for b in range(count)
    ]
    staged = [
        pltpu.make_async_copy(
            query_weight.at[pl.ds(t * part, part), :], stage.at[t], stage_sems.at[t]
        )
        for t in range(sections)
    ]
    direct = [
        pltpu.make_async_copy(stage.at[t], out.at[t, pl.ds(0, part), :], direct_sems.at[t])
        for t in range(sections)
    ]
    for copy in loads + blocks + staged:
        copy.start()
    rows16[...] = jnp.zeros_like(rows16)
    factor = gain[...].astype(F32).reshape(1, part)
    for copy in loads:
        copy.wait()
    both_weights = jnp.concatenate([keyval_weight[0], keyval_weight[1]], axis=1)
    for b in range(count):
        blocks[b].wait()
        staged[b].wait()
        direct[b].start()
        block = x[b * size : (b + 1) * size, :].astype(F32)
        total = jnp.sum(block * block, axis=1, keepdims=True)
        line = jnp.transpose(jnp.broadcast_to(total, (size, size)))[0:1, :]
        high = line.astype(BF16).astype(F32)
        rows16[b : b + 1, :] = high
        rows16[count + b : count + b + 1, :] = line - high
        block = block * factor
        high = block.astype(BF16)
        low = (block - high.astype(F32)).astype(BF16)
        both = jnp.dot(
            jnp.concatenate([high, low], axis=0), both_weights, preferred_element_type=F32
        )
        both = (both[:size] + both[size:]).astype(BF16)
        tail[b, 0:size, :] = both[:, :width]
        tail[b, size : 2 * size, :] = both[:, width:]
    for t in range(sections):
        tail[t, 2 * size : 2 * size + 16, :] = rows16[...].astype(BF16)
    last = pltpu.make_async_copy(tail, out.at[:, pl.ds(part, 2 * size + 16), :], tail_sem)
    last.start()
    for copy in direct + [last]:
        copy.wait()


def partial_kernel(sections, place, x, gain, arrived, cosine, sine, out, squares, normed):
    rows, part = x.shape
    size = BLOCK
    count = rows // size
    head_width = arrived.shape[2]
    tail = jnp.sum(arrived[:, part + 2 * size : part + 2 * size + 16, :].astype(F32), axis=0)
    squares[0:count, :] = lax.rsqrt(
        (tail[0:count, :] + tail[count : 2 * count, :]) / (part * sections) + EPSILON
    )
    for b in range(count):
        scale = spread_down(squares[b : b + 1, :], size)
        scale = jnp.concatenate([scale] * (part // size), axis=1)
        block = x[b * size : (b + 1) * size, :].astype(F32) * scale * gain[...].astype(F32)
        normed[b * size : (b + 1) * size, :] = block.astype(BF16)
    for k in range(0, sections, 2):
        pair = jnp.concatenate([arrived[k, 0:part, :], arrived[k + 1, 0:part, :]], axis=1)
        value = jnp.dot(normed[...], pair, preferred_element_type=F32).astype(BF16)
        out[k, 0:rows, :] = value[:, :head_width]
        out[k + 1, 0:rows, :] = value[:, head_width:]
    scale = spread_down(squares[pl.ds(place[0], 1), :], size)
    keys = jnp.sum(arrived[:, part : part + size, :].astype(F32), axis=0)
    keys = turn(keys * scale, cosine[...], sine[...]).astype(BF16)
    values = jnp.sum(arrived[:, part + size : part + 2 * size, :].astype(F32), axis=0)
    values = (values * scale).astype(BF16)
    for target in range(sections):
        out[target, rows : rows + size, :] = keys
        out[target, rows + size : rows + 2 * size, :] = values


def finish_kernel(header_ids, arrived, cosine, sine, queries, keyval, picked):
    rows, head_width = queries.shape
    size = BLOCK
    count = rows // size
    for b in range(count):
        part = slice(b * size, (b + 1) * size)
        total = jnp.sum(arrived[:, part, :].astype(F32), axis=0)
        queries[part, :] = turn(total, cosine[part, :], sine[part, :]).astype(BF16)
        keyval[part, 0:head_width] = arrived[b, rows : rows + size, :]
        keyval[part, head_width:] = arrived[b, rows + size : rows + 2 * size, :]
    for h in range(picked.shape[0] // size):
        start = pl.multiple_of(lax.rem(header_ids[h], count) * size, size)
        picked[h * size : (h + 1) * size, 0:head_width] = queries[pl.ds(start, size), :]
        picked[h * size : (h + 1) * size, head_width:] = keyval[pl.ds(start, size), :]


def repeat_kernel(seq_place, header_ids, local_blocks, spread, out):
    header = lax.div(seq_place[0] * spread.shape[1], BLOCK)
    rows = spread[lax.div(header_ids[header], local_blocks[0])]
    out[...] = jnp.broadcast_to(rows[None], out.shape)


def window_kernel(
    total_blocks, seq_place, reach, header_ids, queries, before, here, after, header, out
):
    rows, head_width = queries.shape
    size = BLOCK
    count = rows // size
    parts = [before[j * size : (j + 1) * size, :] for j in range(REACH)]
    parts += [here[j * size : (j + 1) * size, :] for j in range(count)]
    parts += [after[j * size : (j + 1) * size, :] for j in range(REACH)]
    head_keys = header[:, head_width : 2 * head_width]
    head_values = header[:, 2 * head_width :]
    for b in range(count):
        near = parts[b : b + 2 * REACH + 1]
        keys = jnp.concatenate([part[:, :head_width] for part in near] + [head_keys], axis=0)
        values = jnp.concatenate([part[:, head_width:] for part in near] + [head_values], axis=0)
        scores = lax.dot_general(
            queries[b * size : (b + 1) * size, :],
            keys,
            (((1,), (1,)), ((), ())),
            preferred_element_type=F32,
        ) * (1.0 / math.sqrt(head_width))
        pieces = []
        for j in range(2 * REACH + 1):
            block = seq_place[0] * count + b + j - REACH
            allowed = (block >= 0) & (block < total_blocks) & (abs(j - REACH) <= reach[b])
            for h in range(2):
                allowed = allowed & (block != header_ids[h])
            pieces.append(
                jnp.where(allowed, scores[:, j * size : (j + 1) * size], -jnp.inf)
            )
        pieces.append(scores[:, (2 * REACH + 1) * size :])
        scores = jnp.concatenate(pieces, axis=1)
        weights = jnp.exp(scores - jnp.max(scores, axis=1, keepdims=True))
        total = jnp.sum(weights, axis=1, keepdims=True)
        mixed = jnp.dot(weights.astype(BF16), values, preferred_element_type=F32)
        out[b * size : (b + 1) * size, :] = (mixed / total).astype(BF16)


def far_kernel(header, keyval, out):
    head_width = header.shape[1] // 3
    scores = lax.dot_general(
        header[:, 0:head_width],
        keyval[:, 0:head_width],
        (((1,), (1,)), ((), ())),
        preferred_element_type=F32,
    ) * (1.0 / math.sqrt(head_width))
    top = jnp.max(scores, axis=1, keepdims=True)
    weights = jnp.exp(scores - top)
    total = jnp.sum(weights, axis=1, keepdims=True)
    mixed = jnp.dot(weights.astype(BF16), keyval[:, head_width:], preferred_element_type=F32)
    level = jnp.broadcast_to(top + jnp.log(total), mixed.shape)
    first = level.astype(BF16).astype(F32)
    second = (level - first).astype(BF16).astype(F32)
    lane = lax.broadcasted_iota(jnp.int32, mixed.shape, 1)
    level = jnp.where(lane < 32, first, jnp.where(lane < 64, second, level - first - second))
    out[:, 0:head_width] = (mixed / total).astype(BF16)
    out[:, head_width:] = level.astype(BF16)


def place_kernel(seq_place, header_ids, attended, weight, _, out, block, semaphore):
    size = BLOCK
    count = out.shape[0] // size
    for h in range(2):

        @pl.when(lax.div(header_ids[h], count) == seq_place[0])
        def _():
            rows = slice(h * size, (h + 1) * size)
            left = jnp.concatenate(
                [attended[s, rows, :] for s in range(attended.shape[0])], axis=1
            )
            block[...] = jnp.dot(left, weight[...], preferred_element_type=F32).astype(BF16)
            start = pl.multiple_of(lax.rem(header_ids[h], count) * size, size)
            copy = pltpu.make_async_copy(block, out.at[pl.ds(start, size), :], semaphore)
            copy.start()
            copy.wait()


def merge_kernel(parts, out):
    head_width = out.shape[2]
    everything = parts[...].astype(F32)
    level = everything[:, :, head_width:]
    level = level[:, :, 0:1] + level[:, :, 32:33] + level[:, :, 64:65]
    factor = jnp.exp(level - jnp.max(level, axis=0, keepdims=True))
    total = jnp.sum(everything[:, :, :head_width] * factor, axis=0)
    result = (total / jnp.sum(factor, axis=0)).astype(BF16)
    out[...] = jnp.broadcast_to(result[None], out.shape)


def on_device(
    hidden,
    norm_gain,
    query_weight,
    key_weight,
    value_weight,
    output_weight,
    block_reach,
    header_ids,
):
    bf16, f32 = jnp.bfloat16, jnp.float32
    rows, part = hidden.shape
    head_width = key_weight.shape[1]
    sections = lax.axis_size("section")
    shards = lax.axis_size("seq")
    local_blocks = rows // BLOCK
    total_blocks = local_blocks * shards
    section_place = lax.axis_index("section")
    seq_place = lax.axis_index("seq")
    headers = header_ids.shape[0]
    mine = headers * BLOCK // shards
    gain = norm_gain[None, :]

    places = [place.astype(jnp.int32).reshape(1) for place in (section_place, seq_place)]
    tall = part + 2 * BLOCK + 16
    hbm = pl.BlockSpec(memory_space=pltpu.HBM)
    outgoing = pl.pallas_call(
        functools.partial(outgoing_kernel, sections),
        out_shape=jax.ShapeDtypeStruct((sections, tall, head_width), bf16),
        in_specs=[pl.BlockSpec(memory_space=pltpu.VMEM)] + [hbm] * 4,
        out_specs=hbm,
        scratch_shapes=[
            pltpu.VMEM((rows, part), bf16),
            pltpu.VMEM((2, part, head_width), bf16),
            pltpu.VMEM((sections, part, head_width), bf16),
            pltpu.VMEM((sections, 2 * BLOCK + 16, head_width), bf16),
            pltpu.VMEM((16, head_width), f32),
            pltpu.SemaphoreType.DMA((local_blocks,)),
            pltpu.SemaphoreType.DMA((2,)),
            pltpu.SemaphoreType.DMA((sections,)),
            pltpu.SemaphoreType.DMA((sections,)),
            pltpu.SemaphoreType.DMA,
        ],
    )(norm_gain, hidden, query_weight, key_weight, value_weight)
    incoming = lax.all_to_all(outgoing, "section", 0, 0)
    own_positions = seq_place * rows + jnp.arange(rows, dtype=jnp.int32)
    own_tables = tables(own_positions, head_width)
    block_tables = [
        lax.dynamic_slice_in_dim(table, section_place * BLOCK, BLOCK, axis=0)
        for table in own_tables
    ]
    (payload,) = call(
        functools.partial(partial_kernel, sections),
        [((sections, rows + 2 * BLOCK, head_width), bf16)],
        [places[0]],
        [hidden, gain, incoming, *block_tables],
        [pltpu.VMEM((8, head_width), f32), pltpu.VMEM((rows, part), bf16)],
    )
    arrived = lax.all_to_all(payload, "section", 0, 0)
    queries, stacked, picked = call(
        finish_kernel,
        [
            ((rows, head_width), bf16),
            ((rows, 2 * head_width), bf16),
            ((headers * BLOCK, 3 * head_width), bf16),
        ],
        [header_ids],
        [arrived, *own_tables],
    )

    spread = lax.all_to_all(picked.reshape(shards, mine, 3 * head_width), "seq", 0, 0)
    (header_copies,) = call(
        repeat_kernel,
        [((shards, mine, 3 * head_width), bf16)],
        [places[1], header_ids, jnp.full((1,), local_blocks, jnp.int32)],
        [spread],
    )
    margin_rows = REACH * BLOCK
    before = shift(stacked[rows - margin_rows :], "seq", 1)
    header_copies, edges, before = lax.optimization_barrier((header_copies, stacked, before))
    header_pack = lax.all_to_all(header_copies, "seq", 0, 0).reshape(-1, 3 * head_width)
    after = shift(edges[:margin_rows], "seq", -1)
    (partial,) = call(
        far_kernel,
        [((headers * BLOCK, 2 * head_width), bf16)],
        [],
        [header_pack, stacked],
    )
    partial, queries, after = lax.optimization_barrier((partial, queries, after))
    parts = lax.all_to_all(partial.reshape(shards, mine, 2 * head_width), "seq", 0, 0)
    everywhere = sections * shards
    (mixed,) = call(
        functools.partial(window_kernel, total_blocks),
        [((rows, head_width), bf16)],
        [places[1], block_reach, header_ids],
        [queries, before, stacked, after, header_pack],
    )
    (result_copies,) = call(
        merge_kernel, [((everywhere, mine, head_width), bf16)], [], [parts]
    )
    result_copies, mixed = lax.optimization_barrier((result_copies, mixed))
    header_all = lax.all_to_all(result_copies, ("section", "seq"), 0, 0).reshape(
        sections, headers * BLOCK, head_width
    )
    gathered = lax.all_gather(mixed, "section", axis=1, tiled=True)
    result = jnp.dot(gathered, output_weight, preferred_element_type=f32).astype(bf16)
    whole = pl.BlockSpec(memory_space=pltpu.VMEM)
    scalar = pl.BlockSpec(memory_space=pltpu.SMEM)
    anywhere = pl.BlockSpec(memory_space=pl.ANY)
    return pl.pallas_call(
        place_kernel,
        out_shape=jax.ShapeDtypeStruct(result.shape, bf16),
        in_specs=[scalar, scalar, whole, whole, anywhere],
        out_specs=anywhere,
        scratch_shapes=[pltpu.VMEM((BLOCK, result.shape[1]), bf16), pltpu.SemaphoreType.DMA],
        input_output_aliases={4: 0},
        compiler_params=pltpu.CompilerParams(vmem_limit_bytes=VMEM_LIMIT),
    )(places[1], header_ids, header_all, output_weight, result)


def solution(mesh):
    return jax.shard_map(
        on_device,
        mesh=mesh,
        in_specs=(
            P("seq", "section"),
            P("section"),
            P(None, "section"),
            P("section", None),
            P("section", None),
            P(None, "section"),
            P("seq"),
            P(),
        ),
        out_specs=P("seq", "section"),
        check_vma=False,
    )
```

```python
import functools
import math

import jax
import jax.numpy as jnp
from jax import lax
from jax.experimental import pallas as pl
from jax.experimental.pallas import tpu as pltpu
from jax.sharding import PartitionSpec as P

BLOCK = 128
REACH = 2

EPSILON = 1e-05
THETA = 500000.0


def shift(value, axis, by):
    count = lax.axis_size(axis)
    return lax.ppermute(value, axis, [(i, (i + by) % count) for i in range(count)])


def tables(positions, head_width):
    middle = head_width // 2
    frequency = jnp.exp(
        -(2.0 / head_width) * math.log(THETA) * jnp.arange(middle, dtype=jnp.float32)
    )
    angles = positions.astype(jnp.float32)[:, None] * frequency[None, :]
    cosine, sine = jnp.cos(angles), jnp.sin(angles)
    return jnp.concatenate([cosine, cosine], axis=1), jnp.concatenate([-sine, sine], axis=1)

BF16, F32 = jnp.bfloat16, jnp.float32
VMEM_LIMIT = 24 * 1024 * 1024


def call(kernel, outs, scalars, arrays, scratch=()):
    whole = pl.BlockSpec(memory_space=pltpu.VMEM)
    specs = [pl.BlockSpec(memory_space=pltpu.SMEM)] * len(scalars)
    specs += [whole] * len(arrays)
    return pl.pallas_call(
        kernel,
        out_shape=[jax.ShapeDtypeStruct(shape, dtype) for shape, dtype in outs],
        in_specs=specs,
        out_specs=[whole] * len(outs),
        scratch_shapes=list(scratch),
        compiler_params=pltpu.CompilerParams(vmem_limit_bytes=VMEM_LIMIT),
    )(*scalars, *arrays)


def turn(values, cosine, signed_sine):
    return values * cosine + pltpu.roll(values, values.shape[1] // 2, axis=1) * signed_sine


def spread_down(row, size):
    return jnp.transpose(jnp.broadcast_to(row, (size, size)))


def outgoing_kernel(
    sections,
    gain,
    hidden,
    query_weight,
    key_weight,
    value_weight,
    out,
    x,
    keyval_weight,
    stage,
    tail,
    rows16,
    block_sems,
    weight_sems,
    stage_sems,
    direct_sems,
    tail_sem,
):
    rows, part = x.shape
    size = BLOCK
    count = rows // size
    width = key_weight.shape[1]
    loads = [
        pltpu.make_async_copy(key_weight, keyval_weight.at[0], weight_sems.at[0]),
        pltpu.make_async_copy(value_weight, keyval_weight.at[1], weight_sems.at[1]),
    ]
    blocks = [
        pltpu.make_async_copy(
            hidden.at[pl.ds(b * size, size), :], x.at[pl.ds(b * size, size), :], block_sems.at[b]
        )
        for b in range(count)
    ]
    staged = [
        pltpu.make_async_copy(
            query_weight.at[pl.ds(t * part, part), :], stage.at[t], stage_sems.at[t]
        )
        for t in range(sections)
    ]
    direct = [
        pltpu.make_async_copy(stage.at[t], out.at[t, pl.ds(0, part), :], direct_sems.at[t])
        for t in range(sections)
    ]
    for copy in loads + blocks + staged:
        copy.start()
    rows16[...] = jnp.zeros_like(rows16)
    factor = gain[...].astype(F32).reshape(1, part)
    for copy in loads:
        copy.wait()
    both_weights = jnp.concatenate([keyval_weight[0], keyval_weight[1]], axis=1)
    for b in range(count):
        blocks[b].wait()
        staged[b].wait()
        direct[b].start()
        block = x[b * size : (b + 1) * size, :].astype(F32)
        total = jnp.sum(block * block, axis=1, keepdims=True)
        line = jnp.transpose(jnp.broadcast_to(total, (size, size)))[0:1, :]
        high = line.astype(BF16).astype(F32)
        rows16[b : b + 1, :] = high
        rows16[count + b : count + b + 1, :] = line - high
        block = block * factor
        high = block.astype(BF16)
        low = (block - high.astype(F32)).astype(BF16)
        both = jnp.dot(
            jnp.concatenate([high, low], axis=0), both_weights, preferred_element_type=F32
        )
        both = (both[:size] + both[size:]).astype(BF16)
        tail[b, 0:size, :] = both[:, :width]
        tail[b, size : 2 * size, :] = both[:, width:]
    for t in range(sections):
        tail[t, 2 * size : 2 * size + 16, :] = rows16[...].astype(BF16)
    last = pltpu.make_async_copy(tail, out.at[:, pl.ds(part, 2 * size + 16), :], tail_sem)
    last.start()
    for copy in direct + [last]:
        copy.wait()


def partial_kernel(sections, place, x, gain, arrived, cosine, sine, out, squares, normed):
    rows, part = x.shape
    size = BLOCK
    count = rows // size
    head_width = arrived.shape[2]
    tail = jnp.sum(arrived[:, part + 2 * size : part + 2 * size + 16, :].astype(F32), axis=0)
    squares[0:count, :] = lax.rsqrt(
        (tail[0:count, :] + tail[count : 2 * count, :]) / (part * sections) + EPSILON
    )
    for b in range(count):
        scale = spread_down(squares[b : b + 1, :], size)
        scale = jnp.concatenate([scale] * (part // size), axis=1)
        block = x[b * size : (b + 1) * size, :].astype(F32) * scale * gain[...].astype(F32)
        normed[b * size : (b + 1) * size, :] = block.astype(BF16)
    for k in range(0, sections, 2):
        pair = jnp.concatenate([arrived[k, 0:part, :], arrived[k + 1, 0:part, :]], axis=1)
        value = jnp.dot(normed[...], pair, preferred_element_type=F32).astype(BF16)
        out[k, 0:rows, :] = value[:, :head_width]
        out[k + 1, 0:rows, :] = value[:, head_width:]
    scale = spread_down(squares[pl.ds(place[0], 1), :], size)
    keys = jnp.sum(arrived[:, part : part + size, :].astype(F32), axis=0)
    keys = turn(keys * scale, cosine[...], sine[...]).astype(BF16)
    values = jnp.sum(arrived[:, part + size : part + 2 * size, :].astype(F32), axis=0)
    values = (values * scale).astype(BF16)
    for target in range(sections):
        out[target, rows : rows + size, :] = keys
        out[target, rows + size : rows + 2 * size, :] = values


def finish_kernel(header_ids, arrived, cosine, sine, queries, keyval, picked):
    rows, head_width = queries.shape
    size = BLOCK
    count = rows // size
    for b in range(count):
        part = slice(b * size, (b + 1) * size)
        total = jnp.sum(arrived[:, part, :].astype(F32), axis=0)
        queries[part, :] = turn(total, cosine[part, :], sine[part, :]).astype(BF16)
        keyval[part, 0:head_width] = arrived[b, rows : rows + size, :]
        keyval[part, head_width:] = arrived[b, rows + size : rows + 2 * size, :]
    for h in range(picked.shape[0] // size):
        start = pl.multiple_of(lax.rem(header_ids[h], count) * size, size)
        picked[h * size : (h + 1) * size, 0:head_width] = queries[pl.ds(start, size), :]
        picked[h * size : (h + 1) * size, head_width:] = keyval[pl.ds(start, size), :]


def repeat_kernel(seq_place, header_ids, local_blocks, spread, out, own, semaphore):
    header = lax.div(seq_place[0] * spread.shape[1], BLOCK)
    owner = lax.div(header_ids[header], local_blocks[0])
    copy = pltpu.make_async_copy(spread.at[owner], own, semaphore)
    copy.start()
    copy.wait()
    out[...] = jnp.broadcast_to(own[...][None], out.shape)


def window_kernel(
    total_blocks, seq_place, reach, header_ids, queries, before, here, after, header, out
):
    rows, head_width = queries.shape
    size = BLOCK
    count = rows // size
    parts = [before[j * size : (j + 1) * size, :] for j in range(REACH)]
    parts += [here[j * size : (j + 1) * size, :] for j in range(count)]
    parts += [after[j * size : (j + 1) * size, :] for j in range(REACH)]
    head_keys = header[:, head_width : 2 * head_width]
    head_values = header[:, 2 * head_width :]
    for b in range(count):
        near = parts[b : b + 2 * REACH + 1]
        keys = jnp.concatenate([part[:, :head_width] for part in near] + [head_keys], axis=0)
        values = jnp.concatenate([part[:, head_width:] for part in near] + [head_values], axis=0)
        scores = lax.dot_general(
            queries[b * size : (b + 1) * size, :],
            keys,
            (((1,), (1,)), ((), ())),
            preferred_element_type=F32,
        ) * (1.0 / math.sqrt(head_width))
        pieces = []
        for j in range(2 * REACH + 1):
            block = seq_place[0] * count + b + j - REACH
            allowed = (block >= 0) & (block < total_blocks) & (abs(j - REACH) <= reach[b])
            for h in range(2):
                allowed = allowed & (block != header_ids[h])
            pieces.append(
                jnp.where(allowed, scores[:, j * size : (j + 1) * size], -jnp.inf)
            )
        pieces.append(scores[:, (2 * REACH + 1) * size :])
        scores = jnp.concatenate(pieces, axis=1)
        weights = jnp.exp(scores - jnp.max(scores, axis=1, keepdims=True))
        total = jnp.sum(weights, axis=1, keepdims=True)
        mixed = jnp.dot(weights.astype(BF16), values, preferred_element_type=F32)
        out[b * size : (b + 1) * size, :] = (mixed / total).astype(BF16)


def far_kernel(header, keyval, out):
    head_width = header.shape[1] // 3
    scores = lax.dot_general(
        header[:, 0:head_width],
        keyval[:, 0:head_width],
        (((1,), (1,)), ((), ())),
        preferred_element_type=F32,
    ) * (1.0 / math.sqrt(head_width))
    top = jnp.max(scores, axis=1, keepdims=True)
    weights = jnp.exp(scores - top)
    total = jnp.sum(weights, axis=1, keepdims=True)
    mixed = jnp.dot(weights.astype(BF16), keyval[:, head_width:], preferred_element_type=F32)
    level = jnp.broadcast_to(top + jnp.log(total), mixed.shape)
    first = level.astype(BF16).astype(F32)
    second = (level - first).astype(BF16).astype(F32)
    lane = lax.broadcasted_iota(jnp.int32, mixed.shape, 1)
    level = jnp.where(lane < 32, first, jnp.where(lane < 64, second, level - first - second))
    out[:, 0:head_width] = (mixed / total).astype(BF16)
    out[:, head_width:] = level.astype(BF16)


def place_kernel(seq_place, header_ids, attended, weight, _, out, block, semaphore):
    size = BLOCK
    count = out.shape[0] // size
    for h in range(2):

        @pl.when(lax.div(header_ids[h], count) == seq_place[0])
        def _():
            rows = slice(h * size, (h + 1) * size)
            left = jnp.concatenate(
                [attended[s, rows, :] for s in range(attended.shape[0])], axis=1
            )
            block[...] = jnp.dot(left, weight[...], preferred_element_type=F32).astype(BF16)
            start = pl.multiple_of(lax.rem(header_ids[h], count) * size, size)
            copy = pltpu.make_async_copy(block, out.at[pl.ds(start, size), :], semaphore)
            copy.start()
            copy.wait()


def merge_kernel(parts, out):
    head_width = out.shape[2]
    everything = parts[...].astype(F32)
    level = everything[:, :, head_width:]
    level = level[:, :, 0:1] + level[:, :, 32:33] + level[:, :, 64:65]
    factor = jnp.exp(level - jnp.max(level, axis=0, keepdims=True))
    total = jnp.sum(everything[:, :, :head_width] * factor, axis=0)
    result = (total / jnp.sum(factor, axis=0)).astype(BF16)
    out[...] = jnp.broadcast_to(result[None], out.shape)


def on_device(
    hidden,
    norm_gain,
    query_weight,
    key_weight,
    value_weight,
    output_weight,
    block_reach,
    header_ids,
):
    bf16, f32 = jnp.bfloat16, jnp.float32
    rows, part = hidden.shape
    head_width = key_weight.shape[1]
    sections = lax.axis_size("section")
    shards = lax.axis_size("seq")
    local_blocks = rows // BLOCK
    total_blocks = local_blocks * shards
    section_place = lax.axis_index("section")
    seq_place = lax.axis_index("seq")
    headers = header_ids.shape[0]
    mine = headers * BLOCK // shards
    gain = norm_gain[None, :]

    places = [place.astype(jnp.int32).reshape(1) for place in (section_place, seq_place)]
    tall = part + 2 * BLOCK + 16
    hbm = pl.BlockSpec(memory_space=pltpu.HBM)
    outgoing = pl.pallas_call(
        functools.partial(outgoing_kernel, sections),
        out_shape=jax.ShapeDtypeStruct((sections, tall, head_width), bf16),
        in_specs=[pl.BlockSpec(memory_space=pltpu.VMEM)] + [hbm] * 4,
        out_specs=hbm,
        scratch_shapes=[
            pltpu.VMEM((rows, part), bf16),
            pltpu.VMEM((2, part, head_width), bf16),
            pltpu.VMEM((sections, part, head_width), bf16),
            pltpu.VMEM((sections, 2 * BLOCK + 16, head_width), bf16),
            pltpu.VMEM((16, head_width), f32),
            pltpu.SemaphoreType.DMA((local_blocks,)),
            pltpu.SemaphoreType.DMA((2,)),
            pltpu.SemaphoreType.DMA((sections,)),
            pltpu.SemaphoreType.DMA((sections,)),
            pltpu.SemaphoreType.DMA,
        ],
    )(norm_gain, hidden, query_weight, key_weight, value_weight)
    incoming = lax.all_to_all(outgoing, "section", 0, 0)
    own_positions = seq_place * rows + jnp.arange(rows, dtype=jnp.int32)
    own_tables = tables(own_positions, head_width)
    block_tables = [
        lax.dynamic_slice_in_dim(table, section_place * BLOCK, BLOCK, axis=0)
        for table in own_tables
    ]
    (payload,) = call(
        functools.partial(partial_kernel, sections),
        [((sections, rows + 2 * BLOCK, head_width), bf16)],
        [places[0]],
        [hidden, gain, incoming, *block_tables],
        [pltpu.VMEM((8, head_width), f32), pltpu.VMEM((rows, part), bf16)],
    )
    arrived = lax.all_to_all(payload, "section", 0, 0)
    queries, stacked, picked = call(
        finish_kernel,
        [
            ((rows, head_width), bf16),
            ((rows, 2 * head_width), bf16),
            ((headers * BLOCK, 3 * head_width), bf16),
        ],
        [header_ids],
        [arrived, *own_tables],
    )

    spread = lax.all_to_all(picked.reshape(shards, mine, 3 * head_width), "seq", 0, 0)
    scalar = pl.BlockSpec(memory_space=pltpu.SMEM)
    header_copies = pl.pallas_call(
        repeat_kernel,
        out_shape=jax.ShapeDtypeStruct(spread.shape, bf16),
        in_specs=[scalar] * 3 + [pl.BlockSpec(memory_space=pl.ANY)],
        out_specs=pl.BlockSpec(memory_space=pltpu.VMEM),
        scratch_shapes=[pltpu.VMEM(spread.shape[1:], bf16), pltpu.SemaphoreType.DMA],
        compiler_params=pltpu.CompilerParams(vmem_limit_bytes=VMEM_LIMIT),
    )(places[1], header_ids, jnp.full((1,), local_blocks, jnp.int32), spread)
    margin_rows = REACH * BLOCK
    before = shift(stacked[rows - margin_rows :], "seq", 1)
    header_copies, edges, before = lax.optimization_barrier((header_copies, stacked, before))
    header_pack = lax.all_to_all(header_copies, "seq", 0, 0).reshape(-1, 3 * head_width)
    after = shift(edges[:margin_rows], "seq", -1)
    (partial,) = call(
        far_kernel,
        [((headers * BLOCK, 2 * head_width), bf16)],
        [],
        [header_pack, stacked],
    )
    partial, queries, after = lax.optimization_barrier((partial, queries, after))
    parts = lax.all_to_all(partial.reshape(shards, mine, 2 * head_width), "seq", 0, 0)
    everywhere = sections * shards
    (mixed,) = call(
        functools.partial(window_kernel, total_blocks),
        [((rows, head_width), bf16)],
        [places[1], block_reach, header_ids],
        [queries, before, stacked, after, header_pack],
    )
    (result_copies,) = call(
        merge_kernel, [((everywhere, mine, head_width), bf16)], [], [parts]
    )
    result_copies, mixed = lax.optimization_barrier((result_copies, mixed))
    header_all = lax.all_to_all(result_copies, ("section", "seq"), 0, 0).reshape(
        sections, headers * BLOCK, head_width
    )
    gathered = lax.all_gather(mixed, "section", axis=1, tiled=True)
    result = jnp.dot(gathered, output_weight, preferred_element_type=f32).astype(bf16)
    whole = pl.BlockSpec(memory_space=pltpu.VMEM)
    scalar = pl.BlockSpec(memory_space=pltpu.SMEM)
    anywhere = pl.BlockSpec(memory_space=pl.ANY)
    return pl.pallas_call(
        place_kernel,
        out_shape=jax.ShapeDtypeStruct(result.shape, bf16),
        in_specs=[scalar, scalar, whole, whole, anywhere],
        out_specs=anywhere,
        scratch_shapes=[pltpu.VMEM((BLOCK, result.shape[1]), bf16), pltpu.SemaphoreType.DMA],
        input_output_aliases={4: 0},
        compiler_params=pltpu.CompilerParams(vmem_limit_bytes=VMEM_LIMIT),
    )(places[1], header_ids, header_all, output_weight, result)


def solution(mesh):
    return jax.shard_map(
        on_device,
        mesh=mesh,
        in_specs=(
            P("seq", "section"),
            P("section"),
            P(None, "section"),
            P("section", None),
            P("section", None),
            P(None, "section"),
            P("seq"),
            P(),
        ),
        out_specs=P("seq", "section"),
        check_vma=False,
    )
```
